32 devices in a mesh: gx: 4 (over x, core), gy: 2 (over y), gz: 4 (over z).
Axes of the slice: x: 2, y: 2, z: 4, core: 2. Of those that a mesh axis runs over, the one named last changes fastest.
Arguments:
- state: float32 [4, 96, 128, 512], P(None, 'gz', 'gx', 'gy'), may hold values from -5 to 5
- mixing: float32 [2, 96, 128, 512], P(None, 'gz', 'gx', 'gy'), may hold values from 0.1 to 1000
- depth_levels: int32 [128, 512], replicated, may hold values from 0 to 96
- wind: float32 [2, 128, 512], P(None, 'gx', 'gy'), may hold values from -3 to 3
Outputs:
- state_next: float32 [4, 96, 128, 512], P(None, 'gz', 'gx', 'gy')
The draws below stay inside these ranges and needn't reach their ends.
Inputs may be any that keep to these rules, and one draw needn't show every extreme that they name: `depth_levels`: levels at or beyond a column's count are land.
All inputs are finite; a program needn't handle non-finite values.
Results may differ from the reference program's by a relative error of at most 0.0003.
Values sent between devices are 32-bit elements; how exact they have to be, the bound alone decides.
A program may use at most 192 MiB of HBM per device.

```python
import math
import jax
import jax.numpy as jnp
from jax import lax

NZ = 96
NX = 128
NY = 512


def place_ends(drawn, key, low, top_value):
    place = [jax.random.randint(jax.random.fold_in(key, axis), (), 0, length) for axis, length in enumerate(drawn.shape)]
    widest = drawn.shape.index(max(drawn.shape))
    next_to = place[:widest] + [(place[widest] + 1) % drawn.shape[widest]] + place[widest + 1:]
    return drawn.at[tuple(place)].set(low).at[tuple(next_to)].set(top_value)


def block_scale(stream_key, dims, pieces, least, high):
    loudness = 1.0
    for dim, blocks in pieces:
        draws = jax.random.uniform(jax.random.fold_in(jax.random.fold_in(stream_key, 6), dim), (blocks,), jnp.float32, least / len(pieces), high / len(pieces))
        loudness = loudness * jnp.repeat(jnp.exp(draws), dims[dim] // blocks).reshape((-1,) + (1,) * (len(dims) - 1 - dim))
    return loudness


def gaussian(own_key, extent, scale, bound, pieces=(), held_as=jnp.bfloat16):
    level = block_scale(own_key, extent, pieces, -0.22, 0.18) if pieces else 1.0
    array = jax.random.normal(own_key, extent, jnp.float32) * scale * level
    return jnp.minimum(jnp.maximum(array, -bound), bound).astype(held_as)


def setup_inputs(seed: int = 0) -> dict:
    seeds = jax.random.split(jax.random.key(seed), 5)
    return {
        "state": gaussian(seeds[0], (4, NZ, NX, NY), 1.0, 5.0, ((1, 4), (2, 4), (3, 2)), jnp.float32),
        "mixing": jnp.clip(jnp.exp(math.log(1000.0) - 9.2103404 * jax.random.uniform(seeds[1], (2, NZ, NX, NY), jnp.float32) ** block_scale(seeds[1], (2, NZ, NX, NY), ((1, 4), (2, 4), (3, 2)), -0.2, 0.2)), 0.1, 1000.0),
        "depth_levels": place_ends(jax.random.randint(seeds[2], (NX, NY), 0, NZ + 1), jax.random.fold_in(seeds[2], 1), 0, NZ).astype(jnp.int32),
        "wind": gaussian(seeds[3], (2, NX, NY), 0.5, 3.0, ((1, 4), (2, 2)), jnp.float32),
    }


def density_of(fields, wet_mask):
    return (-0.3 * fields[0] + 0.7 * fields[1] - 0.05 * fields[0] * fields[0]) * wet_mask


def advance(padded, wet_pad, pressure, wall_face, coriolis):
    wet_x = wet_pad[:, :-1, 1:-1] * wet_pad[:, 1:, 1:-1]
    wet_y = wet_pad[:, 1:-1, :-1] * wet_pad[:, 1:-1, 1:] * wall_face
    east_vel = 0.5 * (padded[2, :, :-1, 1:-1] + padded[2, :, 1:, 1:-1]) * wet_x
    north_vel = 0.5 * (padded[3, :, 1:-1, :-1] + padded[3, :, 1:-1, 1:]) * wet_y
    west_side = padded[:, :, :-1, 1:-1]
    east_side = padded[:, :, 1:, 1:-1]
    flux_x = 0.25 * (jnp.maximum(east_vel, 0.0) * west_side + jnp.minimum(east_vel, 0.0) * east_side) - 0.08 * wet_x * (east_side - west_side)
    south_side = padded[:, :, 1:-1, :-1]
    north_side = padded[:, :, 1:-1, 1:]
    flux_y = 0.25 * (jnp.maximum(north_vel, 0.0) * south_side + jnp.minimum(north_vel, 0.0) * north_side) - 0.08 * wet_y * (north_side - south_side)
    interior = padded[:, :, 1:-1, 1:-1]
    moved = interior - (flux_x[:, :, 1:] - flux_x[:, :, :-1] + flux_y[:, :, :, 1:] - flux_y[:, :, :, :-1])
    centre = pressure[:, 1:-1, 1:-1]
    grad_x = 0.5 * (wet_x[:, 1:] * (pressure[:, 2:, 1:-1] - centre) + wet_x[:, :-1] * (centre - pressure[:, :-2, 1:-1]))
    grad_y = 0.5 * (wet_y[:, :, 1:] * (pressure[:, 1:-1, 2:] - centre) + wet_y[:, :, :-1] * (centre - pressure[:, 1:-1, :-2]))
    east_new = moved[2] + 0.3 * coriolis * interior[3] - grad_x
    north_new = moved[3] - 0.3 * coriolis * interior[2] - grad_y
    wet_inner = wet_pad[:, 1:-1, 1:-1]
    return jnp.stack([moved[0], moved[1], east_new, north_new]) * wet_inner


def tridiagonal(forced, coupling):
    below = jnp.repeat(coupling, 2, axis=0)
    above = jnp.concatenate([jnp.zeros_like(below[:, :1]), below[:, :-1]], axis=1)
    rhs_lev = jnp.moveaxis(forced, 1, 0)
    below_lev = jnp.moveaxis(below, 1, 0)
    above_lev = jnp.moveaxis(above, 1, 0)

    def forward(carry, item):
        ratio_prev, value_prev = carry
        rhs_here, below_here, above_here = item
        divisor = 1.0 + above_here * (1.0 - ratio_prev) + below_here
        ratio = below_here / divisor
        value = (rhs_here + above_here * value_prev) / divisor
        return (ratio, value), (ratio, value)

    zero_level = jnp.zeros_like(rhs_lev[0])
    _, (ratios, values) = lax.scan(forward, (zero_level, zero_level), (rhs_lev, below_lev, above_lev), unroll=8)

    def backward(later, item):
        ratio, value = item
        result = value + ratio * later
        return result, result

    _, solved = lax.scan(backward, zero_level, (ratios, values), reverse=True, unroll=8)
    return jnp.moveaxis(solved, 0, 1)


def reference(state, mixing, depth_levels, wind):
    levels = jnp.arange(NZ, dtype=jnp.int32)
    wet = (levels[:, None, None] < depth_levels[None]).astype(jnp.float32)
    wet_next = ((levels + 1)[:, None, None] < depth_levels[None]).astype(jnp.float32)
    density_field = density_of(state, wet)
    pressure = 0.03 * (jnp.cumsum(density_field, axis=0) - 0.5 * density_field)
    padded = jnp.pad(state, ((0, 0), (0, 0), (1, 1), (1, 1)), mode="wrap")
    wet_pad = jnp.pad(wet, ((0, 0), (1, 1), (1, 1)), mode="wrap")
    pressure_pad = jnp.pad(pressure, ((0, 0), (1, 1), (1, 1)), mode="wrap")
    face_row = jnp.arange(NY + 1, dtype=jnp.int32) - 1
    wall_face = ((face_row >= 0) & (face_row <= NY - 2)).astype(jnp.float32)
    coriolis = 0.5 + (jnp.arange(NY, dtype=jnp.int32).astype(jnp.float32) + 0.5) / NY
    forced = advance(padded, wet_pad, pressure_pad, wall_face, coriolis)
    top_level = (levels == 0).astype(jnp.float32)
    forced = forced.at[2:].add(wind[:, None] * top_level[None, :, None, None] * wet[None])
    coupling = mixing * (wet * wet_next)[None]
    return tridiagonal(forced, coupling)
```

```python
import functools

import jax
import jax.numpy as jnp
from jax import lax
from jax.experimental import pallas as pl
from jax.experimental.pallas import tpu as pltpu
from jax.sharding import PartitionSpec as P

MESH = pl.DeviceIdType.MESH
F32 = jnp.float32


def density_of(t, s):
    return t * (-0.3 - 0.05 * t) + 0.7 * s


def as_float(mask):
    return jnp.where(mask, 1.0, 0.0).astype(F32)


def kernel(
    sizes, state, mixing, dep_ref, wind_ref, out,
    st, mx, fr, rat, inv, hx_src, hx, hy_src, hy, south_flux, edge_p,
    s_src, s_in, s_acc, h_src, h_in, h_acc,
    c_out, c_in, mh, h_out, r_in, k_in, k_out, k_a, k_b, d_last,
    st_sem, mx_sem, out_sem, hx_send, hx_recv, hy_send, hy_recv,
    s_send, s_recv, h_send, h_recv, c_send, c_recv, m_send, m_recv, r_send, r_recv, x_send,
):
    gx_n, gy_n, gz_n = sizes
    _, levels, cols, rows = st.shape
    total_x, total_y = dep_ref.shape
    blocks = rows // 128
    half = gz_n // 2
    ix, iy, z = lax.axis_index("gx"), lax.axis_index("gy"), lax.axis_index("gz")
    east, west = lax.rem(ix + 1, gx_n), lax.rem(ix + gx_n - 1, gx_n)
    has_north, has_south = iy < gy_n - 1, iy > 0
    down = z < half
    step = jnp.where(down, 1, -1)
    first = jnp.where(down, 0, levels - 1)
    final = jnp.where(down, levels - 1, 0)
    has_out = (z > 0) & (z < gz_n - 1)
    mid = (z == half - 1) | (z == half)
    base = z * levels

    loads = [pltpu.make_async_copy(state.at[f], st.at[f], st_sem.at[f]) for f in range(4)]
    for copy in loads:
        copy.start()
    load_mx = pltpu.make_async_copy(mixing, mx, mx_sem)
    load_mx.start()

    barrier = pltpu.get_barrier_semaphore()
    for other in (east, west):
        pl.semaphore_signal(barrier, inc=1, device_id={"gx": other}, device_id_type=MESH)
    for d in range(1, gz_n):
        pl.semaphore_signal(barrier, inc=1, device_id={"gz": lax.rem(z + d, gz_n)}, device_id_type=MESH)

    @pl.when(has_north)
    def _():
        pl.semaphore_signal(barrier, inc=1, device_id={"gy": iy + 1}, device_id_type=MESH)

    @pl.when(has_south)
    def _():
        pl.semaphore_signal(barrier, inc=1, device_id={"gy": iy - 1}, device_id_type=MESH)

    greeted = 2 + (gz_n - 1) + jnp.where(has_north, 1, 0) + jnp.where(has_south, 1, 0)
    pl.semaphore_wait(barrier, greeted)

    def remote(src, dst, send, recv, **device):
        return pltpu.make_async_remote_copy(
            src_ref=src, dst_ref=dst, send_sem=send, recv_sem=recv, device_id=device, device_id_type=MESH
        )

    def mixing_copy(target):
        return remote(mixing.at[:, levels - 1], mh, m_send, m_recv, gz=target)

    sends_mixing = (z >= half) & (z < gz_n - 1)

    @pl.when(sends_mixing)
    def _():
        mixing_copy(z + 1).start()

    lane = lax.broadcasted_iota(jnp.int32, (cols, 128), 1)
    lane_wide = lax.broadcasted_iota(jnp.int32, (cols, rows), 1)
    row_wide = lax.broadcasted_iota(jnp.int32, (cols, rows), 0)

    for copy in loads:
        copy.wait()

    def rows_out(k, carry):
        for f in range(4):
            hx_src[0, f, pl.ds(k, 1), :] = st[f, k, cols - 1:cols, :]
            hx_src[1, f, pl.ds(k, 1), :] = st[f, k, 0:1, :]
        return carry

    lax.fori_loop(0, levels, rows_out, 0)
    x_copies = [
        remote(hx_src.at[0], hx.at[0], hx_send.at[0], hx_recv.at[0], gx=east),
        remote(hx_src.at[1], hx.at[1], hx_send.at[1], hx_recv.at[1], gx=west),
    ]
    for copy in x_copies:
        copy.start()

    y_copies = [
        remote(hy_src.at[0], hy.at[0], hy_send.at[0], hy_recv.at[0], gy=lax.rem(iy + 1, gy_n)),
        remote(hy_src.at[1], hy.at[1], hy_send.at[1], hy_recv.at[1], gy=lax.rem(iy + gy_n - 1, gy_n)),
    ]
    zero = jnp.zeros((cols, 128), F32)

    def pack(side):
        def one(k, packed):
            shift = k + 1 if side == 0 else k
            lanes = pl.ds(rows - 128, 128) if side == 0 else pl.ds(0, 128)
            return tuple(
                jnp.where(lane == k, pltpu.roll(st[f, k, :, lanes], shift, 1), packed[f]) for f in range(4)
            )

        packed = lax.fori_loop(0, levels, one, (zero,) * 4)
        for f in range(4):
            hy_src[side, f] = packed[f]

    for side, present, absent_in in ((0, has_north, 1), (1, has_south, 0)):

        @pl.when(present)
        def _(side=side):
            pack(side)
            y_copies[side].start()

        @pl.when(jnp.logical_not(present))
        def _(side=side, absent_in=absent_in):
            for f in range(4):
                hy_src[side, f] = zero
                hy[absent_in, f] = zero

    start_x = pl.multiple_of(ix * cols, cols)
    start_y = pl.multiple_of(iy * rows, rows)
    dep = dep_ref[pl.ds(start_x, cols), pl.ds(start_y, rows)]
    dep_w = dep_ref[pl.ds(lax.rem(start_x + total_x - 1, total_x), 1), pl.ds(start_y, rows)]
    dep_e = dep_ref[pl.ds(lax.rem(start_x + cols, total_x), 1), pl.ds(start_y, rows)]
    block_s = pl.multiple_of(lax.rem(start_y + total_y - 128, total_y), 128)
    block_n = pl.multiple_of(lax.rem(start_y + rows, total_y), 128)
    dep_s = dep_ref[pl.ds(start_x, cols), pl.ds(block_s, 128)][:, 127:128]
    dep_n = dep_ref[pl.ds(start_x, cols), pl.ds(block_n, 128)][:, 0:1]
    dep_s = jnp.where(has_south, dep_s, 0)
    dep_n = jnp.where(has_north, dep_n, 0)

    def from_east(array, row):
        return jnp.where(row_wide == cols - 1, row, pltpu.roll(array, cols - 1, 0))

    def from_west(array, row):
        return jnp.where(row_wide == 0, row, pltpu.roll(array, 1, 0))

    def from_north(array, block):
        wide = jnp.concatenate([block] * blocks, axis=1)
        return jnp.where(lane_wide == rows - 1, wide, pltpu.roll(array, rows - 1, 1))

    def from_south(array, block):
        wide = jnp.concatenate([block] * blocks, axis=1)
        return jnp.where(lane_wide == 0, wide, pltpu.roll(array, 1, 1))

    least_e = jnp.minimum(dep, from_east(dep, dep_e))
    least_n = jnp.minimum(dep, from_north(dep, jnp.broadcast_to(dep_n, (cols, 128))))
    least_w = jnp.minimum(dep[0:1], dep_w)

    def total_one(k, total):
        return total + density_of(st[0, k], st[1, k]) * as_float(base + k < dep)

    s_src[...] = lax.fori_loop(0, levels, total_one, jnp.zeros((cols, rows), F32))

    def s_copy(d, slot):
        return remote(s_src, s_in.at[slot], s_send.at[d - 1], s_recv.at[slot], gz=lax.rem(z + d, gz_n))

    def h_copy(d, slot):
        return remote(h_src, h_in.at[slot], h_send.at[d - 1], h_recv.at[slot], gz=lax.rem(z + d, gz_n))

    for d in range(1, gz_n):

        @pl.when(z + d < gz_n)
        def _(d=d):
            s_copy(d, z).start()

    load_mx.wait()
    slot_in = jnp.where(mid, 1, 0)
    inward = jnp.clip(z + step, 0, gz_n - 1)
    outward = jnp.clip(z - step, 0, gz_n - 1)
    other_z = lax.rem(z + 1, gz_n)

    def below(m):
        return mx[m, levels - 1] * as_float(base + levels < dep)

    for m in range(2):
        d_last[m] = jnp.ones((cols, rows), F32)

    @pl.when(has_out)
    def _():
        remote(c_out, c_in.at[0], c_send, c_recv.at[0], gz=other_z).wait_recv()
        for m in range(2):
            into = c_in[0, m]

            @pl.when(down)
            def _(m=m, into=into):
                k_in[m] = jnp.ones((cols, rows), F32)
                d_last[m] = 1.0 + into

            @pl.when(jnp.logical_not(down))
            def _(m=m, into=into):
                c = below(m)
                ratio = c / (into + c)
                k_in[m] = ratio
                d_last[m] = 1.0 + ratio * into

    def coefficient(t, ds):
        k = first + step * t
        ci = jnp.where(down, k, k - 1)
        wet = as_float(base + ci + 1 < dep)
        new = []
        for m in range(2):
            c = mx[m, ci] * wet
            over = 1.0 / (ds[m] + c)
            ratio = c * over
            rat[m, k] = ratio
            inv[m, k] = over
            new.append(1.0 + ratio * ds[m])
        return tuple(new)

    ds = lax.fori_loop(0, levels - 1, coefficient, (d_last[0], d_last[1]))
    for m in range(2):
        d_last[m] = ds[m]

    @pl.when(down)
    def _():
        for m in range(2):
            c = below(m)
            ratio = c / (d_last[m] + c)
            k_out[m] = ratio
            c_out[m] = ratio * d_last[m]

    @pl.when(jnp.logical_not(down))
    def _():
        for m in range(2):
            k_out[m] = jnp.ones((cols, rows), F32)
            c_out[m] = d_last[m]

    c_copy = remote(c_out, c_in.at[slot_in], c_send, c_recv.at[slot_in], gz=inward)
    c_copy.start()

    for copy in x_copies:
        copy.wait_recv()

    @pl.when(has_south)
    def _():
        y_copies[0].wait_recv()

    @pl.when(has_north)
    def _():
        y_copies[1].wait_recv()

    def total_rows(k, totals):
        at = pl.ds(k, 1)
        w = density_of(hx[0, 0, at, :], hx[0, 1, at, :]) * as_float(base + k < dep_w)
        e = density_of(hx[1, 0, at, :], hx[1, 1, at, :]) * as_float(base + k < dep_e)
        return totals[0] + w, totals[1] + e

    row_zero = jnp.zeros((1, rows), F32)
    tot_w, tot_e = lax.fori_loop(0, levels, total_rows, (row_zero, row_zero))

    lane_level = jnp.where(lane < levels, base + lane, 1 << 20)

    def running(dens):
        sh = 1
        while sh < levels:
            dens = dens + jnp.where(lane >= sh, pltpu.roll(dens, sh, 1), 0.0)
            sh *= 2
        return dens

    dens_n = density_of(hy[1, 0], hy[1, 1]) * as_float(lane_level < dep_n)
    dens_s = density_of(hy[0, 0], hy[0, 1]) * as_float(lane_level < dep_s)
    dens_o = density_of(hy_src[1, 0], hy_src[1, 1]) * as_float(lane_level < dep[:, 0:1])
    tot_n = jnp.sum(dens_n, axis=1, keepdims=True)
    tot_s = jnp.sum(dens_s, axis=1, keepdims=True)
    h_src[0:cols, :] = jnp.where(lane == 0, tot_s, jnp.where(lane == 1, tot_n, 0.0))
    for b in range(blocks):
        part = slice(b * 128, b * 128 + 128)
        at = cols + 8 * b
        h_src[at:at + 8, :] = jnp.concatenate([tot_w[:, part], tot_e[:, part], jnp.zeros((6, 128), F32)], axis=0)

    for d in range(1, gz_n):

        @pl.when(z + d < gz_n)
        def _(d=d):
            h_copy(d, z).start()

    s_acc[...] = jnp.zeros_like(s_acc)
    h_acc[...] = jnp.zeros_like(h_acc)
    for p in range(gz_n - 1):

        @pl.when(z > p)
        def _(p=p):
            s_copy(1, p).wait_recv()
            s_acc[...] = s_acc[...] + s_in[p]
            h_copy(1, p).wait_recv()
            h_acc[...] = h_acc[...] + h_in[p]

    edge_p[0] = h_acc[0:cols, 1:2] + running(dens_n) - 0.5 * dens_n
    p_s = h_acc[0:cols, 0:1] + running(dens_s) - 0.5 * dens_s
    p_o = s_acc[:, 0:1] + running(dens_o) - 0.5 * dens_o
    mask_s = as_float(lane_level < jnp.minimum(dep_s, dep[:, 0:1]))
    edge_p[1] = mask_s * (p_o - p_s)
    vel = 0.5 * (hy[0, 3] + hy_src[1, 3]) * mask_s
    take_s = 0.25 * jnp.maximum(vel, 0.0) + 0.08 * mask_s
    take_n = 0.25 * jnp.minimum(vel, 0.0) - 0.08 * mask_s
    for f in range(4):
        south_flux[f] = take_s * hy[0, f] + take_n * hy_src[1, f]

    sign = jnp.where(down, 1.0, -1.0).astype(F32)
    own = jnp.where(down, 0.0, 1.0).astype(F32)

    def wide_row(ref, r):
        return jnp.concatenate([ref[cols + 8 * b + r:cols + 8 * b + r + 1, :] for b in range(blocks)], axis=1)

    run = s_acc[...] + own * s_src[...]
    run_w = wide_row(h_acc, 0) + own * wide_row(h_src, 0)
    run_e = wide_row(h_acc, 1) + own * wide_row(h_src, 1)
    coriolis = 0.3 * (0.5 + ((start_y + lane_wide).astype(F32) + 0.5) / total_y)

    def advance(t, carry):
        run, run_w, run_e = carry
        k = first + step * t
        kg = base + k
        at = pl.ds(k, 1)
        c = [st[f, k] for f in range(4)]
        w = [hx[0, f, at, :] for f in range(4)]
        e = [hx[1, f, at, :] for f in range(4)]
        to_north = 127 - k
        to_south = lax.rem(128 - k, 128)
        wet = as_float(kg < dep)
        mask_x = as_float(kg < least_e)
        mask_y = as_float(kg < least_n)
        mask_w = as_float(kg < least_w)
        c_e = [from_east(c[f], e[f]) for f in range(4)]
        c_n = [from_north(c[f], pltpu.roll(hy[1, f], to_north, 1)) for f in range(4)]

        def takes(vel, mask):
            return 0.25 * jnp.maximum(vel, 0.0) + 0.08 * mask, 0.25 * jnp.minimum(vel, 0.0) - 0.08 * mask

        ax, bx = takes(0.5 * (c[2] + c_e[2]) * mask_x, mask_x)
        aw, bw = takes(0.5 * (w[2] + c[2][0:1]) * mask_w, mask_w)
        ay, by = takes(0.5 * (c[3] + c_n[3]) * mask_y, mask_y)
        moved = []
        for f in range(4):
            flux_x = ax * c[f] + bx * c_e[f]
            flux_y = ay * c[f] + by * c_n[f]
            flux_w = from_west(flux_x, aw * w[f] + bw * c[f][0:1])
            flux_s = from_south(flux_y, pltpu.roll(south_flux[f], to_south, 1))
            moved.append(c[f] - (flux_x - flux_w + flux_y - flux_s))

        dens = density_of(c[0], c[1]) * wet
        dens_w = density_of(w[0], w[1]) * as_float(kg < dep_w)
        dens_e = density_of(e[0], e[1]) * as_float(kg < dep_e)
        p = run + (0.5 * sign) * dens
        p_w = run_w + (0.5 * sign) * dens_w
        p_e = run_e + (0.5 * sign) * dens_e
        g_x = mask_x * (from_east(p, p_e) - p)
        g_y = mask_y * (from_north(p, pltpu.roll(edge_p[0], to_north, 1)) - p)
        g_x = g_x + from_west(g_x, mask_w * (p[0:1] - p_w))
        g_y = g_y + from_south(g_y, pltpu.roll(edge_p[1], to_south, 1))
        top = jnp.where(kg == 0, 1.0, 0.0).astype(F32)
        fr[0, k] = moved[0] * wet
        fr[1, k] = moved[1] * wet
        fr[2, k] = (moved[2] + coriolis * c[3] - 0.015 * g_x + top * wind_ref[0]) * wet
        fr[3, k] = (moved[3] - coriolis * c[2] - 0.015 * g_y + top * wind_ref[1]) * wet
        return run + sign * dens, run_w + sign * dens_w, run_e + sign * dens_e

    lax.fori_loop(0, levels, advance, (run, run_w, run_e))

    @pl.when(mid)
    def _():
        remote(c_out, c_in.at[1], c_send, c_recv.at[1], gz=other_z).wait_recv()

    receives_mixing = z > half

    @pl.when(receives_mixing)
    def _():
        mixing_copy(other_z).wait_recv()

    for m in range(2):

        @pl.when(down & jnp.logical_not(mid))
        def _(m=m):
            c = below(m)
            over = 1.0 / (d_last[m] + c)
            k_a[m] = over
            k_b[m] = c * over

        @pl.when(receives_mixing)
        def _(m=m):
            c = mh[m] * as_float(base < dep)
            over = 1.0 / (d_last[m] + c)
            k_a[m] = over
            k_b[m] = c * over

        @pl.when(z == half - 1)
        def _(m=m):
            c = below(m)
            ratio = c / (c_in[1, m] + c)
            over = 1.0 / (d_last[m] + ratio * c_in[1, m])
            k_a[m] = over
            k_b[m] = ratio * over

        @pl.when(z == half)
        def _(m=m):
            over = 1.0 / (d_last[m] + c_in[1, m])
            k_a[m] = over
            k_b[m] = over

    in_copies = [remote(h_out.at[f], r_in.at[slot_in, f], r_send.at[f], r_recv.at[slot_in, f], gz=inward) for f in range(4)]
    out_copies = [remote(fr.at[f, first], r_in.at[1, f], x_send.at[f], r_recv.at[1, f], gz=outward) for f in range(4)]
    stores = [pltpu.make_async_copy(fr.at[f], out.at[f], out_sem.at[f]) for f in range(4)]

    for f in range(4):
        m = f // 2

        @pl.when(has_out)
        def _(f=f, m=m):
            remote(h_out.at[f], r_in.at[0, f], r_send.at[f], r_recv.at[0, f], gz=other_z).wait_recv()
            fr[f, first] = fr[f, first] + k_in[m] * r_in[0, f]

        def forward(t, g, f=f, m=m):
            k = first + step * t
            g = fr[f, k] + rat[m, k - step] * g
            fr[f, k] = g
            return g

        g = lax.fori_loop(1, levels, forward, fr[f, first])
        h_out[f] = k_out[m] * g
        in_copies[f].start()

    for f in range(4):
        m = f // 2
        remote(h_out.at[f], r_in.at[1, f], r_send.at[f], r_recv.at[1, f], gz=other_z).wait_recv()
        x = k_a[m] * fr[f, final] + k_b[m] * r_in[1, f]
        fr[f, final] = x

        def backward(t, x, f=f, m=m):
            k = final - step * t
            x = inv[m, k] * fr[f, k] + rat[m, k] * x
            fr[f, k] = x
            return x

        lax.fori_loop(1, levels, backward, x)

        @pl.when(has_out)
        def _(f=f):
            out_copies[f].start()

        stores[f].start()

    for copy in x_copies:
        copy.wait_send()
    for side, present in ((0, has_north), (1, has_south)):

        @pl.when(present)
        def _(side=side):
            y_copies[side].wait_send()

    for d in range(1, gz_n):

        @pl.when(z + d < gz_n)
        def _(d=d):
            s_copy(d, z).wait_send()
            h_copy(d, z).wait_send()

    @pl.when(sends_mixing)
    def _():
        mixing_copy(z + 1).wait_send()

    c_copy.wait_send()
    for f in range(4):
        in_copies[f].wait_send()

        @pl.when(has_out)
        def _(f=f):
            out_copies[f].wait_send()

        stores[f].wait()


def per_device(sizes, state, mixing, depth_levels, wind):
    _, levels, cols, rows = state.shape
    gz_n = sizes[2]
    blocks = rows // 128
    any_spec = pl.BlockSpec(memory_space=pl.ANY)
    vmem_spec = pl.BlockSpec(memory_space=pltpu.VMEM)
    vmem = lambda *shape: pltpu.VMEM(shape, F32)
    dma = lambda *shape: pltpu.SemaphoreType.DMA(shape)
    tile = (cols, rows)
    earlier = max(gz_n - 1, 1)
    h_rows = cols + 8 * blocks
    one = pltpu.SemaphoreType.DMA
    scratch = [
        vmem(4, levels, *tile), vmem(2, levels, *tile), vmem(4, levels, *tile),
        vmem(2, levels, *tile), vmem(2, levels, *tile),
        vmem(2, 4, levels, rows), vmem(2, 4, levels, rows), vmem(2, 4, cols, 128), vmem(2, 4, cols, 128),
        vmem(4, cols, 128), vmem(2, cols, 128),
        vmem(*tile), vmem(earlier, *tile), vmem(*tile),
        vmem(h_rows, 128), vmem(earlier, h_rows, 128), vmem(h_rows, 128),
        vmem(2, *tile), vmem(2, 2, *tile), vmem(2, *tile), vmem(4, *tile), vmem(2, 4, *tile),
        vmem(2, *tile), vmem(2, *tile), vmem(2, *tile), vmem(2, *tile), vmem(2, *tile),
        dma(4), one, dma(4), dma(2), dma(2), dma(2), dma(2),
        dma(earlier), dma(earlier), dma(earlier), dma(earlier), one, dma(2), one, one, dma(4), dma(2, 4), dma(4),
    ]
    return pl.pallas_call(
        functools.partial(kernel, sizes),
        out_shape=jax.ShapeDtypeStruct(state.shape, F32),
        in_specs=[any_spec, any_spec, vmem_spec, vmem_spec],
        out_specs=any_spec,
        scratch_shapes=scratch,
        compiler_params=pltpu.CompilerParams(
            collective_id=0, has_side_effects=True, vmem_limit_bytes=40 * 1024 * 1024
        ),
        cost_estimate=pl.CostEstimate(flops=state.size * 60, bytes_accessed=state.size * 10, transcendentals=0),
    )(state, mixing, depth_levels, wind)


def solution(mesh):
    sizes = tuple(mesh.shape[name] for name in ("gx", "gy", "gz"))
    return jax.shard_map(
        functools.partial(per_device, sizes),
        mesh=mesh,
        in_specs=(P(None, "gz", "gx", "gy"), P(None, "gz", "gx", "gy"), P(), P(None, "gx", "gy")),
        out_specs=P(None, "gz", "gx", "gy"),
        check_vma=False,
    )
```

```python
import functools

import jax
import jax.numpy as jnp
from jax import lax
from jax.experimental import pallas as pl
from jax.experimental.pallas import tpu as pltpu
from jax.sharding import PartitionSpec as P

MESH = pl.DeviceIdType.MESH
F32 = jnp.float32


def density_of(t, s):
    return t * (-0.3 - 0.05 * t) + 0.7 * s


def as_float(mask):
    return jnp.where(mask, 1.0, 0.0).astype(F32)


def kernel(
    sizes, state, mixing, dep_any, wind_any, out,
    dep_ref, wind_ref, st, mx, fr, rat, inv, take, take_w, via, w_last, hx_src, hx, hy_src, hy, south_flux, edge_p,
    s_src, s_in, s_acc, h_src, h_in, h_acc,
    c_out, c_in, mh, h_out, r_in, k_in, k_out, k_a, k_b, d_last,
    dep_sem, wind_sem, st_sem, mx_sem, out_sem, hx_send, hx_recv, hy_send, hy_recv,
    s_send, s_recv, h_send, h_recv, c_send, c_recv, m_send, m_recv, r_send, r_recv, x_send,
):
    gx_n, gy_n, gz_n = sizes
    _, levels, cols, rows = st.shape
    total_x, total_y = dep_any.shape
    blocks = rows // 128
    half = gz_n // 2
    ix, iy, z = lax.axis_index("gx"), lax.axis_index("gy"), lax.axis_index("gz")
    east, west = lax.rem(ix + 1, gx_n), lax.rem(ix + gx_n - 1, gx_n)
    has_north, has_south = iy < gy_n - 1, iy > 0
    down = z < half
    step = jnp.where(down, 1, -1)
    first = jnp.where(down, 0, levels - 1)
    final = jnp.where(down, levels - 1, 0)
    has_out = (z > 0) & (z < gz_n - 1)
    mid = (z == half - 1) | (z == half)
    base = z * levels

    loads = [pltpu.make_async_copy(state.at[f], st.at[f], st_sem.at[f]) for f in range(4)]
    for copy in loads:
        copy.start()
    load_dep = pltpu.make_async_copy(dep_any, dep_ref, dep_sem)
    load_dep.start()
    load_mx = pltpu.make_async_copy(mixing, mx, mx_sem)
    load_mx.start()
    load_wind = pltpu.make_async_copy(wind_any, wind_ref, wind_sem)
    load_wind.start()

    barrier = pltpu.get_barrier_semaphore()
    for other in (east, west):
        pl.semaphore_signal(barrier, inc=1, device_id={"gx": other}, device_id_type=MESH)
    for d in range(1, gz_n):
        pl.semaphore_signal(barrier, inc=1, device_id={"gz": lax.rem(z + d, gz_n)}, device_id_type=MESH)

    @pl.when(has_north)
    def _():
        pl.semaphore_signal(barrier, inc=1, device_id={"gy": iy + 1}, device_id_type=MESH)

    @pl.when(has_south)
    def _():
        pl.semaphore_signal(barrier, inc=1, device_id={"gy": iy - 1}, device_id_type=MESH)

    greeted = 2 + (gz_n - 1) + jnp.where(has_north, 1, 0) + jnp.where(has_south, 1, 0)
    pl.semaphore_wait(barrier, greeted)

    def remote(src, dst, send, recv, **device):
        return pltpu.make_async_remote_copy(
            src_ref=src, dst_ref=dst, send_sem=send, recv_sem=recv, device_id=device, device_id_type=MESH
        )

    def mixing_copy(target):
        return remote(mixing.at[:, levels - 1], mh, m_send, m_recv, gz=target)

    sends_mixing = (z >= half) & (z < gz_n - 1)

    @pl.when(sends_mixing)
    def _():
        mixing_copy(z + 1).start()

    lane = lax.broadcasted_iota(jnp.int32, (cols, 128), 1)
    lane_wide = lax.broadcasted_iota(jnp.int32, (cols, rows), 1)

    for copy in loads:
        copy.wait()

    def rows_out(k, carry):
        for f in range(4):
            hx_src[0, f, pl.ds(k, 1), :] = st[f, k, cols - 1:cols, :]
            hx_src[1, f, pl.ds(k, 1), :] = st[f, k, 0:1, :]
        return carry

    lax.fori_loop(0, levels, rows_out, 0)
    x_copies = [
        remote(hx_src.at[0], hx.at[0], hx_send.at[0], hx_recv.at[0], gx=east),
        remote(hx_src.at[1], hx.at[1], hx_send.at[1], hx_recv.at[1], gx=west),
    ]
    for copy in x_copies:
        copy.start()

    y_copies = [
        remote(hy_src.at[0], hy.at[0], hy_send.at[0], hy_recv.at[0], gy=lax.rem(iy + 1, gy_n)),
        remote(hy_src.at[1], hy.at[1], hy_send.at[1], hy_recv.at[1], gy=lax.rem(iy + gy_n - 1, gy_n)),
    ]
    zero = jnp.zeros((cols, 128), F32)

    def pack(side):
        def one(k, packed):
            shift = k + 1 if side == 0 else k
            lanes = pl.ds(rows - 128, 128) if side == 0 else pl.ds(0, 128)
            return tuple(
                jnp.where(lane == k, pltpu.roll(st[f, k, :, lanes], shift, 1), packed[f]) for f in range(4)
            )

        packed = lax.fori_loop(0, levels, one, (zero,) * 4)
        for f in range(4):
            hy_src[side, f] = packed[f]

    for side, present, absent_in in ((0, has_north, 1), (1, has_south, 0)):

        @pl.when(present)
        def _(side=side):
            pack(side)
            y_copies[side].start()

        @pl.when(jnp.logical_not(present))
        def _(side=side, absent_in=absent_in):
            for f in range(4):
                hy_src[side, f] = zero
                hy[absent_in, f] = zero

    load_dep.wait()
    start_x = pl.multiple_of(ix * cols, cols)
    start_y = pl.multiple_of(iy * rows, rows)
    dep = dep_ref[pl.ds(start_x, cols), pl.ds(start_y, rows)]
    dep_w = dep_ref[pl.ds(lax.rem(start_x + total_x - 1, total_x), 1), pl.ds(start_y, rows)]
    dep_e = dep_ref[pl.ds(lax.rem(start_x + cols, total_x), 1), pl.ds(start_y, rows)]
    block_s = pl.multiple_of(lax.rem(start_y + total_y - 128, total_y), 128)
    block_n = pl.multiple_of(lax.rem(start_y + rows, total_y), 128)
    dep_s = dep_ref[pl.ds(start_x, cols), pl.ds(block_s, 128)][:, 127:128]
    dep_n = dep_ref[pl.ds(start_x, cols), pl.ds(block_n, 128)][:, 0:1]
    dep_s = jnp.where(has_south, dep_s, 0)
    dep_n = jnp.where(has_north, dep_n, 0)

    tile_row = lax.broadcasted_iota(jnp.int32, (8, rows), 0)
    tiles = cols // 8

    def from_east(array, row):
        turned = [pltpu.roll(array[8 * i:8 * i + 8], 7, 0) for i in range(tiles)] + [row]
        return jnp.concatenate([jnp.where(tile_row == 7, turned[i + 1], turned[i]) for i in range(tiles)], axis=0)

    def from_west(array, row):
        turned = [row] + [pltpu.roll(array[8 * i:8 * i + 8], 1, 0) for i in range(tiles)]
        return jnp.concatenate([jnp.where(tile_row == 0, turned[i], turned[i + 1]) for i in range(tiles)], axis=0)

    def from_north(array, block):
        turned = [pltpu.roll(array[:, 128 * b:128 * b + 128], 127, 1) for b in range(blocks)] + [block]
        return jnp.concatenate([jnp.where(lane == 127, turned[b + 1], turned[b]) for b in range(blocks)], axis=1)

    def from_south(array, block):
        turned = [block] + [pltpu.roll(array[:, 128 * b:128 * b + 128], 1, 1) for b in range(blocks)]
        return jnp.concatenate([jnp.where(lane == 0, turned[b], turned[b + 1]) for b in range(blocks)], axis=1)

    least_e = jnp.minimum(dep, from_east(dep, dep_e))
    least_n = jnp.minimum(dep, from_north(dep, jnp.broadcast_to(dep_n, (cols, 128))))
    least_w = jnp.minimum(dep[0:1], dep_w)

    def total_one(k, total):
        return total + density_of(st[0, k], st[1, k]) * as_float(base + k < dep)

    s_src[...] = lax.fori_loop(0, levels, total_one, jnp.zeros((cols, rows), F32))

    def s_copy(d, slot):
        return remote(s_src, s_in.at[slot], s_send.at[d - 1], s_recv.at[slot], gz=lax.rem(z + d, gz_n))

    def h_copy(d, slot):
        return remote(h_src, h_in.at[slot], h_send.at[d - 1], h_recv.at[slot], gz=lax.rem(z + d, gz_n))

    for d in range(1, gz_n):

        @pl.when(z + d < gz_n)
        def _(d=d):
            s_copy(d, z).start()

    load_mx.wait()
    slot_in = jnp.where(mid, 1, 0)
    inward = jnp.clip(z + step, 0, gz_n - 1)
    outward = jnp.clip(z - step, 0, gz_n - 1)
    other_z = lax.rem(z + 1, gz_n)
    c_copy = remote(c_out, c_in.at[slot_in], c_send, c_recv.at[slot_in], gz=inward)

    def below(m):
        return mx[m, levels - 1] * as_float(base + levels < dep)

    def coefficients():
        def coefficient(t, carry):
            k = first + step * t
            ci = jnp.where(down, k, k - 1)
            wet = as_float(base + ci + 1 < dep)
            new = []
            for m in range(2):
                c = mx[m, ci] * wet
                over = 1.0 / (carry[m] + c)
                ratio = c * over
                rat[m, k + step] = ratio
                inv[m, k] = over
                new.append(1.0 + ratio * carry[m])
            via[k] = over * carry[2]
            new.append(ratio * carry[2])
            return tuple(new)

        carry = lax.fori_loop(0, levels - 1, coefficient, (d_last[0], d_last[1], w_last[...]))
        for m in range(2):
            d_last[m] = carry[m]
            rat[m, first] = jnp.zeros((cols, rows), F32)
        w_last[...] = carry[2]

        @pl.when(down)
        def _():
            for m in range(2):
                c = below(m)
                ratio = c / (d_last[m] + c)
                k_out[m] = ratio
                c_out[m] = ratio * d_last[m]

        @pl.when(jnp.logical_not(down))
        def _():
            for m in range(2):
                k_out[m] = jnp.ones((cols, rows), F32)
                c_out[m] = d_last[m]

        c_copy.start()

    @pl.when(jnp.logical_not(has_out))
    def _():
        for m in range(2):
            d_last[m] = jnp.ones((cols, rows), F32)
            r_in[0, 2 + m] = jnp.zeros((cols, rows), F32)
        w_last[...] = jnp.zeros((cols, rows), F32)
        coefficients()

    for copy in x_copies:
        copy.wait_recv()

    @pl.when(has_south)
    def _():
        y_copies[0].wait_recv()

    @pl.when(has_north)
    def _():
        y_copies[1].wait_recv()

    def total_rows(k, totals):
        at = pl.ds(k, 1)
        w = density_of(hx[0, 0, at, :], hx[0, 1, at, :]) * as_float(base + k < dep_w)
        e = density_of(hx[1, 0, at, :], hx[1, 1, at, :]) * as_float(base + k < dep_e)
        return totals[0] + w, totals[1] + e

    row_zero = jnp.zeros((1, rows), F32)
    tot_w, tot_e = lax.fori_loop(0, levels, total_rows, (row_zero, row_zero))

    lane_level = jnp.where(lane < levels, base + lane, 1 << 20)

    def running(dens):
        sh = 1
        while sh < levels:
            dens = dens + jnp.where(lane >= sh, pltpu.roll(dens, sh, 1), 0.0)
            sh *= 2
        return dens

    dens_n = density_of(hy[1, 0], hy[1, 1]) * as_float(lane_level < dep_n)
    dens_s = density_of(hy[0, 0], hy[0, 1]) * as_float(lane_level < dep_s)
    dens_o = density_of(hy_src[1, 0], hy_src[1, 1]) * as_float(lane_level < dep[:, 0:1])
    tot_n = jnp.sum(dens_n, axis=1, keepdims=True)
    tot_s = jnp.sum(dens_s, axis=1, keepdims=True)
    h_src[0:cols, :] = jnp.where(lane == 0, tot_s, jnp.where(lane == 1, tot_n, 0.0))
    for b in range(blocks):
        part = slice(b * 128, b * 128 + 128)
        at = cols + 8 * b
        h_src[at:at + 8, :] = jnp.concatenate([tot_w[:, part], tot_e[:, part], jnp.zeros((6, 128), F32)], axis=0)

    for d in range(1, gz_n):

        @pl.when(z + d < gz_n)
        def _(d=d):
            h_copy(d, z).start()

    mask_s = as_float(lane_level < jnp.minimum(dep_s, dep[:, 0:1]))

    def takes(vel, mask):
        return 0.25 * jnp.maximum(vel, 0.0) + 0.08 * mask, 0.25 * jnp.minimum(vel, 0.0) - 0.08 * mask

    take_s, take_n = takes(0.5 * (hy[0, 3] + hy_src[1, 3]) * mask_s, mask_s)
    for f in range(4):
        south_flux[f] = take_s * hy[0, f] + take_n * hy_src[1, f]

    def moved_of(f, k, c, w, e, c_e, c_n, ax, bx, ay, by, aw, bw):
        flux_x = ax * c + bx * c_e
        flux_y = ay * c + by * c_n
        flux_w = from_west(flux_x, aw * w + bw * c[0:1])
        flux_s = from_south(flux_y, pltpu.roll(south_flux[f], lax.rem(128 - k, 128), 1))
        return c - (flux_x - flux_w + flux_y - flux_s)

    def advance_tracers(t, carry):
        k = first + step * t
        kg = base + k
        at = pl.ds(k, 1)
        to_north = 127 - k
        mask_x = as_float(kg < least_e)
        mask_y = as_float(kg < least_n)
        mask_w = as_float(kg < least_w)
        u, v = st[2, k], st[3, k]
        ax, bx = takes(0.5 * (u + from_east(u, hx[1, 2, at, :])) * mask_x, mask_x)
        ay, by = takes(0.5 * (v + from_north(v, pltpu.roll(hy[1, 3], to_north, 1))) * mask_y, mask_y)
        aw, bw = takes(0.5 * (hx[0, 2, at, :] + u[0:1]) * mask_w, mask_w)
        take[0, k], take[1, k], take[2, k], take[3, k] = ax, bx, ay, by
        take_w[0, at, :], take_w[1, at, :] = aw, bw
        wet = as_float(kg < dep)
        for f in range(2):
            c, w, e = st[f, k], hx[0, f, at, :], hx[1, f, at, :]
            c_n = from_north(c, pltpu.roll(hy[1, f], to_north, 1))
            fr[f, k] = moved_of(f, k, c, w, e, from_east(c, e), c_n, ax, bx, ay, by, aw, bw) * wet
        return carry

    lax.fori_loop(0, levels, advance_tracers, 0)

    @pl.when(has_out)
    def _():
        remote(c_out, c_in.at[0], c_send, c_recv.at[0], gz=other_z).wait_recv()

        @pl.when(down)
        def _():
            for m in range(2):
                k_in[m] = jnp.ones((cols, rows), F32)
                d_last[m] = 1.0 + c_in[0, m]

        @pl.when(jnp.logical_not(down))
        def _():
            for m in range(2):
                c = below(m)
                ratio = c / (c_in[0, m] + c)
                k_in[m] = ratio
                d_last[m] = 1.0 + ratio * c_in[0, m]

        w_last[...] = k_in[1]
        coefficients()

    in_copies = [remote(h_out.at[f], r_in.at[slot_in, f], r_send.at[f], r_recv.at[slot_in, f], gz=inward) for f in range(4)]
    out_copies = [remote(fr.at[f, first], r_in.at[1, f], x_send.at[f], r_recv.at[1, f], gz=outward) for f in range(4)]
    stores = [pltpu.make_async_copy(fr.at[f], out.at[f], out_sem.at[f]) for f in range(4)]

    def wait_in(slot, f):
        remote(h_out.at[f], r_in.at[slot, f], r_send.at[f], r_recv.at[slot, f], gz=other_z).wait_recv()

    @pl.when(has_out)
    def _():
        for f in range(2):
            wait_in(0, f)
            fr[f, first] = fr[f, first] + k_in[0] * r_in[0, f]

    def forward(t, g):
        k = first + step * t
        ratio = rat[0, k]
        new = tuple(fr[f, k] + ratio * g[f] for f in range(2))
        for f in range(2):
            fr[f, k] = new[f]
        return new

    g = lax.fori_loop(1, levels, forward, (fr[0, first], fr[1, first]))
    for f in range(2):
        h_out[f] = k_out[0] * g[f]
        in_copies[f].start()

    s_acc[...] = jnp.zeros_like(s_acc)
    h_acc[...] = jnp.zeros_like(h_acc)
    for p in range(gz_n - 1):

        @pl.when(z > p)
        def _(p=p):
            s_copy(1, p).wait_recv()
            s_acc[...] = s_acc[...] + s_in[p]
            h_copy(1, p).wait_recv()
            h_acc[...] = h_acc[...] + h_in[p]

    edge_p[0] = h_acc[0:cols, 1:2] + running(dens_n) - 0.5 * dens_n
    p_s = h_acc[0:cols, 0:1] + running(dens_s) - 0.5 * dens_s
    p_o = s_acc[:, 0:1] + running(dens_o) - 0.5 * dens_o
    edge_p[1] = mask_s * (p_o - p_s)

    sign = jnp.where(down, 1.0, -1.0).astype(F32)
    own = jnp.where(down, 0.0, 1.0).astype(F32)

    def wide_row(ref, r):
        return jnp.concatenate([ref[cols + 8 * b + r:cols + 8 * b + r + 1, :] for b in range(blocks)], axis=1)

    run = s_acc[...] + own * s_src[...]
    run_w = wide_row(h_acc, 0) + own * wide_row(h_src, 0)
    run_e = wide_row(h_acc, 1) + own * wide_row(h_src, 1)
    coriolis = 0.3 * (0.5 + ((start_y + lane_wide).astype(F32) + 0.5) / total_y)
    load_wind.wait()

    def advance(t, carry):
        run, run_w, run_e, g_u, g_v = carry
        k = first + step * t
        kg = base + k
        at = pl.ds(k, 1)
        to_north = 127 - k
        to_south = lax.rem(128 - k, 128)
        c = [st[f, k] for f in range(4)]
        w = [hx[0, f, at, :] for f in range(4)]
        e = [hx[1, f, at, :] for f in range(4)]
        wet = as_float(kg < dep)
        mask_x = as_float(kg < least_e)
        mask_y = as_float(kg < least_n)
        mask_w = as_float(kg < least_w)
        coefs = (take[0, k], take[1, k], take[2, k], take[3, k], take_w[0, at, :], take_w[1, at, :])
        moved = [None, None]
        for f in (2, 3):
            c_n = from_north(c[f], pltpu.roll(hy[1, f], to_north, 1))
            moved.append(moved_of(f, k, c[f], w[f], e[f], from_east(c[f], e[f]), c_n, *coefs))
        dens = density_of(c[0], c[1]) * wet
        dens_w = density_of(w[0], w[1]) * as_float(kg < dep_w)
        dens_e = density_of(e[0], e[1]) * as_float(kg < dep_e)
        p = run + (0.5 * sign) * dens
        p_w = run_w + (0.5 * sign) * dens_w
        p_e = run_e + (0.5 * sign) * dens_e
        g_x = mask_x * (from_east(p, p_e) - p)
        g_y = mask_y * (from_north(p, pltpu.roll(edge_p[0], to_north, 1)) - p)
        g_x = g_x + from_west(g_x, mask_w * (p[0:1] - p_w))
        g_y = g_y + from_south(g_y, pltpu.roll(edge_p[1], to_south, 1))
        top = jnp.where(kg == 0, 1.0, 0.0).astype(F32)
        ratio = rat[1, k]
        g_u = (moved[2] + coriolis * c[3] - 0.015 * g_x + top * wind_ref[0]) * wet + ratio * g_u
        g_v = (moved[3] - coriolis * c[2] - 0.015 * g_y + top * wind_ref[1]) * wet + ratio * g_v
        fr[2, k] = g_u
        fr[3, k] = g_v
        return run + sign * dens, run_w + sign * dens_w, run_e + sign * dens_e, g_u, g_v

    wide_zero = jnp.zeros((cols, rows), F32)
    lax.fori_loop(0, levels, advance, (run, run_w, run_e, wide_zero, wide_zero))

    @pl.when(mid)
    def _():
        remote(c_out, c_in.at[1], c_send, c_recv.at[1], gz=other_z).wait_recv()

    receives_mixing = z > half

    @pl.when(receives_mixing)
    def _():
        mixing_copy(other_z).wait_recv()

    for m in range(2):

        @pl.when(down & jnp.logical_not(mid))
        def _(m=m):
            c = below(m)
            over = 1.0 / (d_last[m] + c)
            k_a[m] = over
            k_b[m] = c * over

        @pl.when(receives_mixing)
        def _(m=m):
            c = mh[m] * as_float(base < dep)
            over = 1.0 / (d_last[m] + c)
            k_a[m] = over
            k_b[m] = c * over

        @pl.when(z == half - 1)
        def _(m=m):
            c = below(m)
            ratio = c / (c_in[1, m] + c)
            over = 1.0 / (d_last[m] + ratio * c_in[1, m])
            k_a[m] = over
            k_b[m] = ratio * over

        @pl.when(z == half)
        def _(m=m):
            over = 1.0 / (d_last[m] + c_in[1, m])
            k_a[m] = over
            k_b[m] = over

    def backward_tracers():
        for f in range(2):
            wait_in(1, f)
            fr[f, final] = k_a[0] * fr[f, final] + k_b[0] * r_in[1, f]

        def backward(t, x):
            k = final - step * t
            ratio, over = rat[0, k + step], inv[0, k]
            new = tuple(over * fr[f, k] + ratio * x[f] for f in range(2))
            for f in range(2):
                fr[f, k] = new[f]
            return new

        lax.fori_loop(1, levels, backward, (fr[0, final], fr[1, final]))
        for f in range(2):

            @pl.when(has_out)
            def _(f=f):
                out_copies[f].start()

            stores[f].start()

    @pl.when(has_out)
    def _():
        backward_tracers()
        for f in (2, 3):
            wait_in(0, f)
            fr[f, final] = fr[f, final] + w_last[...] * r_in[0, f]

    for f in (2, 3):
        h_out[f] = k_out[1] * fr[f, final]
        in_copies[f].start()

    @pl.when(jnp.logical_not(has_out))
    def _():
        backward_tracers()

    for f in (2, 3):
        wait_in(1, f)
        fr[f, final] = k_a[1] * fr[f, final] + k_b[1] * r_in[1, f]

    def backward(t, x):
        k = final - step * t
        ratio, over, add = rat[1, k + step], inv[1, k], via[k]
        new = tuple(over * fr[2 + i, k] + ratio * x[i] + add * r_in[0, 2 + i] for i in range(2))
        for i in range(2):
            fr[2 + i, k] = new[i]
        return new

    lax.fori_loop(1, levels, backward, (fr[2, final], fr[3, final]))
    for f in (2, 3):

        @pl.when(has_out)
        def _(f=f):
            out_copies[f].start()

        stores[f].start()

    for copy in x_copies:
        copy.wait_send()
    for side, present in ((0, has_north), (1, has_south)):

        @pl.when(present)
        def _(side=side):
            y_copies[side].wait_send()

    for d in range(1, gz_n):

        @pl.when(z + d < gz_n)
        def _(d=d):
            s_copy(d, z).wait_send()
            h_copy(d, z).wait_send()

    @pl.when(sends_mixing)
    def _():
        mixing_copy(z + 1).wait_send()

    c_copy.wait_send()
    for f in range(4):
        in_copies[f].wait_send()

        @pl.when(has_out)
        def _(f=f):
            out_copies[f].wait_send()

        stores[f].wait()


def per_device(sizes, state, mixing, depth_levels, wind):
    _, levels, cols, rows = state.shape
    gz_n = sizes[2]
    blocks = rows // 128
    any_spec = pl.BlockSpec(memory_space=pl.ANY)
    vmem = lambda *shape: pltpu.VMEM(shape, F32)
    dma = lambda *shape: pltpu.SemaphoreType.DMA(shape)
    tile = (cols, rows)
    earlier = max(gz_n - 1, 1)
    h_rows = cols + 8 * blocks
    one = pltpu.SemaphoreType.DMA
    scratch = [
        pltpu.VMEM(depth_levels.shape, jnp.int32), vmem(2, *tile),
        vmem(4, levels, *tile), vmem(2, levels, *tile), vmem(4, levels, *tile),
        vmem(2, levels, *tile), vmem(2, levels, *tile),
        vmem(4, levels, *tile), vmem(2, levels, rows), vmem(levels, *tile), vmem(*tile),
        vmem(2, 4, levels, rows), vmem(2, 4, levels, rows), vmem(2, 4, cols, 128), vmem(2, 4, cols, 128),
        vmem(4, cols, 128), vmem(2, cols, 128),
        vmem(*tile), vmem(earlier, *tile), vmem(*tile),
        vmem(h_rows, 128), vmem(earlier, h_rows, 128), vmem(h_rows, 128),
        vmem(2, *tile), vmem(2, 2, *tile), vmem(2, *tile), vmem(4, *tile), vmem(2, 4, *tile),
        vmem(2, *tile), vmem(2, *tile), vmem(2, *tile), vmem(2, *tile), vmem(2, *tile),
        one, one, dma(4), one, dma(4), dma(2), dma(2), dma(2), dma(2),
        dma(earlier), dma(earlier), dma(earlier), dma(earlier), one, dma(2), one, one, dma(4), dma(2, 4), dma(4),
    ]
    return pl.pallas_call(
        functools.partial(kernel, sizes),
        out_shape=jax.ShapeDtypeStruct(state.shape, F32),
        in_specs=[any_spec] * 4,
        out_specs=any_spec,
        scratch_shapes=scratch,
        compiler_params=pltpu.CompilerParams(
            collective_id=0, has_side_effects=True, vmem_limit_bytes=60 * 1024 * 1024
        ),
        cost_estimate=pl.CostEstimate(flops=state.size * 60, bytes_accessed=state.size * 10, transcendentals=0),
    )(state, mixing, depth_levels, wind)


def solution(mesh):
    sizes = tuple(mesh.shape[name] for name in ("gx", "gy", "gz"))
    return jax.shard_map(
        functools.partial(per_device, sizes),
        mesh=mesh,
        in_specs=(P(None, "gz", "gx", "gy"), P(None, "gz", "gx", "gy"), P(), P(None, "gx", "gy")),
        out_specs=P(None, "gz", "gx", "gy"),
        check_vma=False,
    )
```

```python
import functools

import jax
import jax.numpy as jnp
from jax import lax
from jax.experimental import pallas as pl
from jax.experimental.pallas import tpu as pltpu
from jax.sharding import PartitionSpec as P

MESH = pl.DeviceIdType.MESH
F32 = jnp.float32


def density_of(t, s):
    return t * (-0.3 - 0.05 * t) + 0.7 * s


def as_float(mask):
    return jnp.where(mask, 1.0, 0.0).astype(F32)


def kernel(
    sizes, state, mixing, dep_any, wind_any, out,
    dep_ref, wind_ref, st, mx, fr, rat, inv, take, take_w, via, w_last, hx_src, hx, hv_src, hv, hy_src, hy, south_flux, edge_p,
    s_src, s_in, s_acc, h_src, h_in, h_acc,
    c_out, c_in, mh, h_out, r_in, k_in, k_out, k_a, k_b, d_last,
    dep_sem, wind_sem, st_sem, mx_sem, out_sem, hx_send, hx_recv, hv_send, hv_recv, hy_send, hy_recv,
    s_send, s_recv, h_send, h_recv, c_send, c_recv, m_send, m_recv, r_send, r_recv, x_send,
):
    gx_n, gy_n, gz_n = sizes
    _, levels, cols, rows = st.shape
    total_x, total_y = dep_any.shape
    blocks = rows // 128
    half = gz_n // 2
    ix, iy, z = lax.axis_index("gx"), lax.axis_index("gy"), lax.axis_index("gz")
    east, west = lax.rem(ix + 1, gx_n), lax.rem(ix + gx_n - 1, gx_n)
    has_north, has_south = iy < gy_n - 1, iy > 0
    down = z < half
    step = jnp.where(down, 1, -1)
    first = jnp.where(down, 0, levels - 1)
    final = jnp.where(down, levels - 1, 0)
    has_out = (z > 0) & (z < gz_n - 1)
    mid = (z == half - 1) | (z == half)
    base = z * levels

    loads = [pltpu.make_async_copy(state.at[f], st.at[f], st_sem.at[f]) for f in range(4)]
    for copy in loads:
        copy.start()
    load_dep = pltpu.make_async_copy(dep_any, dep_ref, dep_sem)
    load_dep.start()
    load_mx = pltpu.make_async_copy(mixing, mx, mx_sem)
    load_mx.start()
    load_wind = pltpu.make_async_copy(wind_any, wind_ref, wind_sem)
    load_wind.start()

    barrier = pltpu.get_barrier_semaphore()
    for other in (east, west):
        pl.semaphore_signal(barrier, inc=1, device_id={"gx": other}, device_id_type=MESH)
    for d in range(1, gz_n):
        pl.semaphore_signal(barrier, inc=1, device_id={"gz": lax.rem(z + d, gz_n)}, device_id_type=MESH)

    @pl.when(has_north)
    def _():
        pl.semaphore_signal(barrier, inc=1, device_id={"gy": iy + 1}, device_id_type=MESH)

    @pl.when(has_south)
    def _():
        pl.semaphore_signal(barrier, inc=1, device_id={"gy": iy - 1}, device_id_type=MESH)

    greeted = 2 + (gz_n - 1) + jnp.where(has_north, 1, 0) + jnp.where(has_south, 1, 0)

    def remote(src, dst, send, recv, **device):
        return pltpu.make_async_remote_copy(
            src_ref=src, dst_ref=dst, send_sem=send, recv_sem=recv, device_id=device, device_id_type=MESH
        )

    lane = lax.broadcasted_iota(jnp.int32, (cols, 128), 1)
    lane_wide = lax.broadcasted_iota(jnp.int32, (cols, rows), 1)

    part = levels // 2

    def rows_out(ch):
        def one(i, carry):
            k = first + step * (ch * part + i)
            for f in range(3):
                hx_src[0, ch, f, pl.ds(i, 1), :] = st[f, k, cols - 1:cols, :]
                hx_src[1, ch, f, pl.ds(i, 1), :] = st[f, k, 0:1, :]
            return carry

        lax.fori_loop(0, part, one, 0)

    x_copies = [
        [
            remote(hx_src.at[0, ch], hx.at[0, ch], hx_send.at[0, ch], hx_recv.at[0, ch], gx=east),
            remote(hx_src.at[1, ch], hx.at[1, ch], hx_send.at[1, ch], hx_recv.at[1, ch], gx=west),
        ]
        for ch in range(2)
    ]
    v_copies = [
        remote(hv_src.at[0], hv.at[0], hv_send.at[0], hv_recv.at[0], gx=east),
        remote(hv_src.at[1], hv.at[1], hv_send.at[1], hv_recv.at[1], gx=west),
    ]
    for copy in loads[:3]:
        copy.wait()
    rows_out(0)
    pl.semaphore_wait(barrier, greeted)
    for copy in x_copies[0]:
        copy.start()

    def mixing_copy(target):
        return remote(mixing.at[:, levels - 1], mh, m_send, m_recv, gz=target)

    sends_mixing = (z >= half) & (z < gz_n - 1)

    @pl.when(sends_mixing)
    def _():
        mixing_copy(z + 1).start()

    loads[3].wait()

    y_copies = [
        remote(hy_src.at[0], hy.at[0], hy_send.at[0], hy_recv.at[0], gy=lax.rem(iy + 1, gy_n)),
        remote(hy_src.at[1], hy.at[1], hy_send.at[1], hy_recv.at[1], gy=lax.rem(iy + gy_n - 1, gy_n)),
    ]
    zero = jnp.zeros((cols, 128), F32)

    def pack(side):
        def one(k, packed):
            shift = k + 1 if side == 0 else k
            lanes = pl.ds(rows - 128, 128) if side == 0 else pl.ds(0, 128)
            return tuple(
                jnp.where(lane == k, pltpu.roll(st[f, k, :, lanes], shift, 1), packed[f]) for f in range(4)
            )

        packed = lax.fori_loop(0, levels, one, (zero,) * 4)
        for f in range(4):
            hy_src[side, f] = packed[f]

    for side, present, absent_in in ((0, has_north, 1), (1, has_south, 0)):

        @pl.when(present)
        def _(side=side):
            pack(side)
            y_copies[side].start()

        @pl.when(jnp.logical_not(present))
        def _(side=side, absent_in=absent_in):
            for f in range(4):
                hy_src[side, f] = zero
                hy[absent_in, f] = zero

    rows_out(1)
    for copy in x_copies[1]:
        copy.start()

    def v_rows(k, carry):
        hv_src[0, pl.ds(k, 1), :] = st[3, k, cols - 1:cols, :]
        hv_src[1, pl.ds(k, 1), :] = st[3, k, 0:1, :]
        return carry

    lax.fori_loop(0, levels, v_rows, 0)
    for copy in v_copies:
        copy.start()

    load_dep.wait()
    start_x = pl.multiple_of(ix * cols, cols)
    start_y = pl.multiple_of(iy * rows, rows)
    dep = dep_ref[pl.ds(start_x, cols), pl.ds(start_y, rows)]
    dep_w = dep_ref[pl.ds(lax.rem(start_x + total_x - 1, total_x), 1), pl.ds(start_y, rows)]
    dep_e = dep_ref[pl.ds(lax.rem(start_x + cols, total_x), 1), pl.ds(start_y, rows)]
    block_s = pl.multiple_of(lax.rem(start_y + total_y - 128, total_y), 128)
    block_n = pl.multiple_of(lax.rem(start_y + rows, total_y), 128)
    dep_s = dep_ref[pl.ds(start_x, cols), pl.ds(block_s, 128)][:, 127:128]
    dep_n = dep_ref[pl.ds(start_x, cols), pl.ds(block_n, 128)][:, 0:1]
    dep_s = jnp.where(has_south, dep_s, 0)
    dep_n = jnp.where(has_north, dep_n, 0)

    tile_row = lax.broadcasted_iota(jnp.int32, (8, rows), 0)
    tiles = cols // 8

    def from_east(array, row):
        turned = [pltpu.roll(array[8 * i:8 * i + 8], 7, 0) for i in range(tiles)] + [row]
        return jnp.concatenate([jnp.where(tile_row == 7, turned[i + 1], turned[i]) for i in range(tiles)], axis=0)

    def from_west(array, row):
        turned = [row] + [pltpu.roll(array[8 * i:8 * i + 8], 1, 0) for i in range(tiles)]
        return jnp.concatenate([jnp.where(tile_row == 0, turned[i], turned[i + 1]) for i in range(tiles)], axis=0)

    def from_north(array, block):
        turned = [pltpu.roll(array[:, 128 * b:128 * b + 128], 127, 1) for b in range(blocks)] + [block]
        return jnp.concatenate([jnp.where(lane == 127, turned[b + 1], turned[b]) for b in range(blocks)], axis=1)

    def from_south(array, block):
        turned = [block] + [pltpu.roll(array[:, 128 * b:128 * b + 128], 1, 1) for b in range(blocks)]
        return jnp.concatenate([jnp.where(lane == 0, turned[b], turned[b + 1]) for b in range(blocks)], axis=1)

    least_e = jnp.minimum(dep, from_east(dep, dep_e))
    least_n = jnp.minimum(dep, from_north(dep, jnp.broadcast_to(dep_n, (cols, 128))))
    least_w = jnp.minimum(dep[0:1], dep_w)

    def total_one(k, total):
        return total + density_of(st[0, k], st[1, k]) * as_float(base + k < dep)

    s_src[...] = lax.fori_loop(0, levels, total_one, jnp.zeros((cols, rows), F32))

    def s_copy(d, slot):
        return remote(s_src, s_in.at[slot], s_send.at[d - 1], s_recv.at[slot], gz=lax.rem(z + d, gz_n))

    def h_copy(d, slot):
        return remote(h_src, h_in.at[slot], h_send.at[d - 1], h_recv.at[slot], gz=lax.rem(z + d, gz_n))

    for d in range(1, gz_n):

        @pl.when(z + d < gz_n)
        def _(d=d):
            s_copy(d, z).start()

    load_mx.wait()
    slot_in = jnp.where(mid, 1, 0)
    inward = jnp.clip(z + step, 0, gz_n - 1)
    outward = jnp.clip(z - step, 0, gz_n - 1)
    other_z = lax.rem(z + 1, gz_n)
    c_copy = remote(c_out, c_in.at[slot_in], c_send, c_recv.at[slot_in], gz=inward)

    def below(m):
        return mx[m, levels - 1] * as_float(base + levels < dep)

    def coefficients():
        def coefficient(t, carry):
            k = first + step * t
            ci = jnp.where(down, k, k - 1)
            wet = as_float(base + ci + 1 < dep)
            new = []
            for m in range(2):
                c = mx[m, ci] * wet
                over = 1.0 / (carry[m] + c)
                ratio = c * over
                rat[m, k + step] = ratio
                inv[m, k] = over
                new.append(1.0 + ratio * carry[m])
            via[k] = over * carry[2]
            new.append(ratio * carry[2])
            return tuple(new)

        carry = lax.fori_loop(0, levels - 1, coefficient, (d_last[0], d_last[1], w_last[...]))
        for m in range(2):
            d_last[m] = carry[m]
            rat[m, first] = jnp.zeros((cols, rows), F32)
        w_last[...] = carry[2]

        @pl.when(down)
        def _():
            for m in range(2):
                c = below(m)
                ratio = c / (d_last[m] + c)
                k_out[m] = ratio
                c_out[m] = ratio * d_last[m]

        @pl.when(jnp.logical_not(down))
        def _():
            for m in range(2):
                k_out[m] = jnp.ones((cols, rows), F32)
                c_out[m] = d_last[m]

        c_copy.start()

    @pl.when(jnp.logical_not(has_out))
    def _():
        for m in range(2):
            d_last[m] = jnp.ones((cols, rows), F32)
            r_in[0, 2 + m] = jnp.zeros((cols, rows), F32)
        w_last[...] = jnp.zeros((cols, rows), F32)
        coefficients()

    for copy in x_copies[0]:
        copy.wait_recv()

    @pl.when(has_south)
    def _():
        y_copies[0].wait_recv()

    @pl.when(has_north)
    def _():
        y_copies[1].wait_recv()

    lane_level = jnp.where(lane < levels, base + lane, 1 << 20)

    wet_s = lane_level < jnp.minimum(dep_s, dep[:, 0:1])

    def takes(both, wet):
        vel = both * jnp.where(wet, 0.125, 0.0).astype(F32)
        near = jnp.maximum(vel, 0.0) + jnp.where(wet, 0.08, 0.0).astype(F32)
        return near, vel - near

    take_s, take_n = takes(hy[0, 3] + hy_src[1, 3], wet_s)
    for f in range(4):
        south_flux[f] = take_s * hy[0, f] + take_n * hy_src[1, f]

    def moved_of(f, k, c, w, e, c_e, c_n, ax, bx, ay, by, aw, bw):
        flux_x = ax * c + bx * c_e
        flux_y = ay * c + by * c_n
        flux_w = from_west(flux_x, aw * w + bw * c[0:1])
        flux_s = from_south(flux_y, pltpu.roll(south_flux[f], lax.rem(128 - k, 128), 1))
        return c - (flux_x - flux_w + flux_y - flux_s)

    def advance_tracers(t, carry, ch):
        k = first + step * t
        ct = pl.ds(t - ch * part, 1)
        kg = base + k
        at = pl.ds(k, 1)
        to_north = 127 - k
        u, v = st[2, k], st[3, k]
        ax, bx = takes(u + from_east(u, hx[1, ch, 2, ct, :]), kg < least_e)
        ay, by = takes(v + from_north(v, pltpu.roll(hy[1, 3], to_north, 1)), kg < least_n)
        aw, bw = takes(hx[0, ch, 2, ct, :] + u[0:1], kg < least_w)
        take[0, k], take[1, k], take[2, k], take[3, k] = ax, bx, ay, by
        take_w[0, at, :], take_w[1, at, :] = aw, bw
        wet = as_float(kg < dep)
        for f in range(2):
            c, w, e = st[f, k], hx[0, ch, f, ct, :], hx[1, ch, f, ct, :]
            c_n = from_north(c, pltpu.roll(hy[1, f], to_north, 1))
            fr[f, k] = moved_of(f, k, c, w, e, from_east(c, e), c_n, ax, bx, ay, by, aw, bw) * wet
        return carry

    lax.fori_loop(0, part, functools.partial(advance_tracers, ch=0), 0)

    for copy in x_copies[1]:
        copy.wait_recv()

    def where_rows(t):
        ch = jnp.where(t < part, 0, 1)
        return ch, pl.ds(t - ch * part, 1)

    def total_rows(t, totals):
        ch, at = where_rows(t)
        k = first + step * t
        w = density_of(hx[0, ch, 0, at, :], hx[0, ch, 1, at, :]) * as_float(base + k < dep_w)
        e = density_of(hx[1, ch, 0, at, :], hx[1, ch, 1, at, :]) * as_float(base + k < dep_e)
        return totals[0] + w, totals[1] + e

    row_zero = jnp.zeros((1, rows), F32)
    tot_w, tot_e = lax.fori_loop(0, levels, total_rows, (row_zero, row_zero))

    def running(dens):
        sh = 1
        while sh < levels:
            dens = dens + jnp.where(lane >= sh, pltpu.roll(dens, sh, 1), 0.0)
            sh *= 2
        return dens

    dens_n = density_of(hy[1, 0], hy[1, 1]) * as_float(lane_level < dep_n)
    dens_s = density_of(hy[0, 0], hy[0, 1]) * as_float(lane_level < dep_s)
    dens_o = density_of(hy_src[1, 0], hy_src[1, 1]) * as_float(lane_level < dep[:, 0:1])
    tot_n = jnp.sum(dens_n, axis=1, keepdims=True)
    tot_s = jnp.sum(dens_s, axis=1, keepdims=True)
    h_src[0:cols, :] = jnp.where(lane == 0, tot_s, jnp.where(lane == 1, tot_n, 0.0))
    for b in range(blocks):
        piece = slice(b * 128, b * 128 + 128)
        at = cols + 8 * b
        h_src[at:at + 8, :] = jnp.concatenate([tot_w[:, piece], tot_e[:, piece], jnp.zeros((6, 128), F32)], axis=0)

    for d in range(1, gz_n):

        @pl.when(z + d < gz_n)
        def _(d=d):
            h_copy(d, z).start()

    lax.fori_loop(part, levels, functools.partial(advance_tracers, ch=1), 0)

    @pl.when(has_out)
    def _():
        remote(c_out, c_in.at[0], c_send, c_recv.at[0], gz=other_z).wait_recv()

        @pl.when(down)
        def _():
            for m in range(2):
                k_in[m] = jnp.ones((cols, rows), F32)
                d_last[m] = 1.0 + c_in[0, m]

        @pl.when(jnp.logical_not(down))
        def _():
            for m in range(2):
                c = below(m)
                ratio = c / (c_in[0, m] + c)
                k_in[m] = ratio
                d_last[m] = 1.0 + ratio * c_in[0, m]

        w_last[...] = k_in[1]
        coefficients()

    in_copies = [remote(h_out.at[f], r_in.at[slot_in, f], r_send.at[f], r_recv.at[slot_in, f], gz=inward) for f in range(4)]
    out_copies = [remote(fr.at[f, first], r_in.at[1, f], x_send.at[f], r_recv.at[1, f], gz=outward) for f in range(4)]
    stores = [pltpu.make_async_copy(fr.at[f], out.at[f], out_sem.at[f]) for f in range(4)]

    def wait_in(slot, f):
        remote(h_out.at[f], r_in.at[slot, f], r_send.at[f], r_recv.at[slot, f], gz=other_z).wait_recv()

    @pl.when(has_out)
    def _():
        for f in range(2):
            wait_in(0, f)
            fr[f, first] = fr[f, first] + k_in[0] * r_in[0, f]

    def forward(t, g):
        k = first + step * t
        ratio = rat[0, k]
        new = tuple(fr[f, k] + ratio * g[f] for f in range(2))
        for f in range(2):
            fr[f, k] = new[f]
        return new

    g = lax.fori_loop(1, levels, forward, (fr[0, first], fr[1, first]))
    for f in range(2):
        h_out[f] = k_out[0] * g[f]
        in_copies[f].start()

    s_acc[...] = jnp.zeros_like(s_acc)
    h_acc[...] = jnp.zeros_like(h_acc)
    for p in range(gz_n - 1):

        @pl.when(z > p)
        def _(p=p):
            s_copy(1, p).wait_recv()
            s_acc[...] = s_acc[...] + s_in[p]
            h_copy(1, p).wait_recv()
            h_acc[...] = h_acc[...] + h_in[p]

    edge_p[0] = h_acc[0:cols, 1:2] + running(dens_n) - 0.5 * dens_n
    p_s = h_acc[0:cols, 0:1] + running(dens_s) - 0.5 * dens_s
    p_o = s_acc[:, 0:1] + running(dens_o) - 0.5 * dens_o
    edge_p[1] = as_float(wet_s) * (p_o - p_s)

    sign = jnp.where(down, 1.0, -1.0).astype(F32)
    own = jnp.where(down, 0.0, 1.0).astype(F32)

    def wide_row(ref, r):
        return jnp.concatenate([ref[cols + 8 * b + r:cols + 8 * b + r + 1, :] for b in range(blocks)], axis=1)

    run = s_acc[...] + own * s_src[...]
    run_w = wide_row(h_acc, 0) + own * wide_row(h_src, 0)
    run_e = wide_row(h_acc, 1) + own * wide_row(h_src, 1)
    coriolis = 0.3 * (0.5 + ((start_y + lane_wide).astype(F32) + 0.5) / total_y)
    load_wind.wait()
    for copy in v_copies:
        copy.wait_recv()

    def advance(t, carry):
        run, run_w, run_e, g_u, g_v = carry
        k = first + step * t
        kg = base + k
        at = pl.ds(k, 1)
        to_north = 127 - k
        to_south = lax.rem(128 - k, 128)
        c = [st[f, k] for f in range(4)]
        ch, ct = where_rows(t)
        w = [hx[0, ch, f, ct, :] for f in range(3)] + [hv[0, at, :]]
        e = [hx[1, ch, f, ct, :] for f in range(3)] + [hv[1, at, :]]
        wet = as_float(kg < dep)
        mask_x = as_float(kg < least_e)
        mask_y = as_float(kg < least_n)
        mask_w = as_float(kg < least_w)
        coefs = (take[0, k], take[1, k], take[2, k], take[3, k], take_w[0, at, :], take_w[1, at, :])
        moved = [None, None]
        for f in (2, 3):
            c_n = from_north(c[f], pltpu.roll(hy[1, f], to_north, 1))
            moved.append(moved_of(f, k, c[f], w[f], e[f], from_east(c[f], e[f]), c_n, *coefs))
        dens = density_of(c[0], c[1]) * wet
        dens_w = density_of(w[0], w[1]) * as_float(kg < dep_w)
        dens_e = density_of(e[0], e[1]) * as_float(kg < dep_e)
        p = run + (0.5 * sign) * dens
        p_w = run_w + (0.5 * sign) * dens_w
        p_e = run_e + (0.5 * sign) * dens_e
        g_x = mask_x * (from_east(p, p_e) - p)
        g_y = mask_y * (from_north(p, pltpu.roll(edge_p[0], to_north, 1)) - p)
        g_x = g_x + from_west(g_x, mask_w * (p[0:1] - p_w))
        g_y = g_y + from_south(g_y, pltpu.roll(edge_p[1], to_south, 1))
        top = jnp.where(kg == 0, 1.0, 0.0).astype(F32)
        ratio = rat[1, k]
        g_u = (moved[2] + coriolis * c[3] - 0.015 * g_x + top * wind_ref[0]) * wet + ratio * g_u
        g_v = (moved[3] - coriolis * c[2] - 0.015 * g_y + top * wind_ref[1]) * wet + ratio * g_v
        fr[2, k] = g_u
        fr[3, k] = g_v
        return run + sign * dens, run_w + sign * dens_w, run_e + sign * dens_e, g_u, g_v

    wide_zero = jnp.zeros((cols, rows), F32)
    lax.fori_loop(0, levels, advance, (run, run_w, run_e, wide_zero, wide_zero))

    @pl.when(mid)
    def _():
        remote(c_out, c_in.at[1], c_send, c_recv.at[1], gz=other_z).wait_recv()

    receives_mixing = z > half

    @pl.when(receives_mixing)
    def _():
        mixing_copy(other_z).wait_recv()

    for m in range(2):

        @pl.when(down & jnp.logical_not(mid))
        def _(m=m):
            c = below(m)
            over = 1.0 / (d_last[m] + c)
            k_a[m] = over
            k_b[m] = c * over

        @pl.when(receives_mixing)
        def _(m=m):
            c = mh[m] * as_float(base < dep)
            over = 1.0 / (d_last[m] + c)
            k_a[m] = over
            k_b[m] = c * over

        @pl.when(z == half - 1)
        def _(m=m):
            c = below(m)
            ratio = c / (c_in[1, m] + c)
            over = 1.0 / (d_last[m] + ratio * c_in[1, m])
            k_a[m] = over
            k_b[m] = ratio * over

        @pl.when(z == half)
        def _(m=m):
            over = 1.0 / (d_last[m] + c_in[1, m])
            k_a[m] = over
            k_b[m] = over

    def backward_tracers():
        for f in range(2):
            wait_in(1, f)
            fr[f, final] = k_a[0] * fr[f, final] + k_b[0] * r_in[1, f]

        def backward(t, x):
            k = final - step * t
            ratio, over = rat[0, k + step], inv[0, k]
            new = tuple(over * fr[f, k] + ratio * x[f] for f in range(2))
            for f in range(2):
                fr[f, k] = new[f]
            return new

        lax.fori_loop(1, levels, backward, (fr[0, final], fr[1, final]))
        for f in range(2):

            @pl.when(has_out)
            def _(f=f):
                out_copies[f].start()

            stores[f].start()

    @pl.when(has_out)
    def _():
        backward_tracers()

    for f in (2, 3):

        @pl.when(has_out)
        def _(f=f):
            wait_in(0, f)
            fr[f, final] = fr[f, final] + w_last[...] * r_in[0, f]

        h_out[f] = k_out[1] * fr[f, final]
        in_copies[f].start()

    @pl.when(jnp.logical_not(has_out))
    def _():
        backward_tracers()

    for f in (2, 3):
        wait_in(1, f)
        came = r_in[0, f]
        x = k_a[1] * fr[f, final] + k_b[1] * r_in[1, f]
        fr[f, final] = x

        def backward(t, x, f=f, came=came):
            k = final - step * t
            x = inv[1, k] * fr[f, k] + rat[1, k + step] * x + via[k] * came
            fr[f, k] = x
            return x

        lax.fori_loop(1, levels, backward, x)

        @pl.when(has_out)
        def _(f=f):
            out_copies[f].start()

        stores[f].start()

    for copy in x_copies[0] + x_copies[1] + v_copies:
        copy.wait_send()
    for side, present in ((0, has_north), (1, has_south)):

        @pl.when(present)
        def _(side=side):
            y_copies[side].wait_send()

    for d in range(1, gz_n):

        @pl.when(z + d < gz_n)
        def _(d=d):
            s_copy(d, z).wait_send()
            h_copy(d, z).wait_send()

    @pl.when(sends_mixing)
    def _():
        mixing_copy(z + 1).wait_send()

    c_copy.wait_send()
    for f in range(4):
        in_copies[f].wait_send()

        @pl.when(has_out)
        def _(f=f):
            out_copies[f].wait_send()

        stores[f].wait()


def place(source, target, held, in_sem, out_sem):
    part = source.shape[1] // 2
    pieces = [(f, h) for f in range(4) for h in range(2)]
    ins = [
        pltpu.make_async_copy(source.at[f, pl.ds(h * part, part)], held.at[f, pl.ds(h * part, part)], in_sem.at[f, h])
        for f, h in pieces
    ]
    outs = [
        pltpu.make_async_copy(held.at[f, pl.ds(h * part, part)], target.at[f, pl.ds(h * part, part)], out_sem.at[f, h])
        for f, h in pieces
    ]
    for copy in ins:
        copy.start()
    for arrived, leaving in zip(ins, outs):
        arrived.wait()
        leaving.start()
    for copy in outs:
        copy.wait()


def per_device(sizes, state, mixing, depth_levels, wind):
    _, levels, cols, rows = state.shape
    gz_n = sizes[2]
    blocks = rows // 128
    any_spec = pl.BlockSpec(memory_space=pl.ANY)
    vmem = lambda *shape: pltpu.VMEM(shape, F32)
    dma = lambda *shape: pltpu.SemaphoreType.DMA(shape)
    tile = (cols, rows)
    earlier = max(gz_n - 1, 1)
    h_rows = cols + 8 * blocks
    one = pltpu.SemaphoreType.DMA
    scratch = [
        pltpu.VMEM(depth_levels.shape, jnp.int32), vmem(2, *tile),
        vmem(4, levels, *tile), vmem(2, levels, *tile), vmem(4, levels, *tile),
        vmem(2, levels, *tile), vmem(2, levels, *tile),
        vmem(4, levels, *tile), vmem(2, levels, rows), vmem(levels, *tile), vmem(*tile),
        vmem(2, 2, 3, levels // 2, rows), vmem(2, 2, 3, levels // 2, rows), vmem(2, levels, rows), vmem(2, levels, rows),
        vmem(2, 4, cols, 128), vmem(2, 4, cols, 128),
        vmem(4, cols, 128), vmem(2, cols, 128),
        vmem(*tile), vmem(earlier, *tile), vmem(*tile),
        vmem(h_rows, 128), vmem(earlier, h_rows, 128), vmem(h_rows, 128),
        vmem(2, *tile), vmem(2, 2, *tile), vmem(2, *tile), vmem(4, *tile), vmem(2, 4, *tile),
        vmem(2, *tile), vmem(2, *tile), vmem(2, *tile), vmem(2, *tile), vmem(2, *tile),
        one, one, dma(4), one, dma(4), dma(2, 2), dma(2, 2), dma(2), dma(2), dma(2), dma(2),
        dma(earlier), dma(earlier), dma(earlier), dma(earlier), one, dma(2), one, one, dma(4), dma(2, 4), dma(4),
    ]
    solved = pl.pallas_call(
        functools.partial(kernel, sizes),
        out_shape=jax.ShapeDtypeStruct(state.shape, F32),
        in_specs=[any_spec] * 4,
        out_specs=any_spec,
        scratch_shapes=scratch,
        compiler_params=pltpu.CompilerParams(
            collective_id=0, has_side_effects=True, vmem_limit_bytes=60 * 1024 * 1024
        ),
        cost_estimate=pl.CostEstimate(flops=state.size * 60, bytes_accessed=state.size * 10, transcendentals=0),
    )(state, mixing, depth_levels, wind)
    return pl.pallas_call(
        place,
        out_shape=jax.ShapeDtypeStruct(state.shape, F32),
        in_specs=[any_spec],
        out_specs=any_spec,
        scratch_shapes=[vmem(*state.shape), dma(4, 2), dma(4, 2)],
        compiler_params=pltpu.CompilerParams(vmem_limit_bytes=60 * 1024 * 1024),
        cost_estimate=pl.CostEstimate(flops=0, bytes_accessed=state.size * 8, transcendentals=0),
    )(solved)


def solution(mesh):
    sizes = tuple(mesh.shape[name] for name in ("gx", "gy", "gz"))
    return jax.shard_map(
        functools.partial(per_device, sizes),
        mesh=mesh,
        in_specs=(P(None, "gz", "gx", "gy"), P(None, "gz", "gx", "gy"), P(), P(None, "gx", "gy")),
        out_specs=P(None, "gz", "gx", "gy"),
        check_vma=False,
    )
```

```python
import functools

import jax
import jax.numpy as jnp
from jax import lax
from jax.experimental import pallas as pl
from jax.experimental.pallas import tpu as pltpu
from jax.sharding import PartitionSpec as P

MESH = pl.DeviceIdType.MESH
F32 = jnp.float32


def density_of(t, s):
    return t * (-0.3 - 0.05 * t) + 0.7 * s


def as_float(mask):
    return jnp.where(mask, 1.0, 0.0).astype(F32)


def kernel(
    sizes, state, mixing, dep_any, wind_any, out,
    dep_ref, wind_ref, st, mx, fr, rat, inv, take, take_w, via, w_last, depths, run_ref, g_ref, hx_src, hx, hv_src, hv, hy_src, hy, south_flux, edge_p,
    s_src, s_in, s_acc, h_src, h_in, h_acc,
    c_out, c_in, mh, h_out, r_in, k_in, k_out, k_a, k_b, d_last,
    dep_sem, wind_sem, st_sem, mx_sem, out_sem, hx_send, hx_recv, hv_send, hv_recv, hy_send, hy_recv,
    s_send, s_recv, h_send, h_recv, c_send, c_recv, m_send, m_recv, r_send, r_recv, x_send,
):
    gx_n, gy_n, gz_n = sizes
    _, levels, cols, rows = st.shape
    total_x, total_y = dep_any.shape
    blocks = rows // 128
    half = gz_n // 2
    ix, iy, z = lax.axis_index("gx"), lax.axis_index("gy"), lax.axis_index("gz")
    east, west = lax.rem(ix + 1, gx_n), lax.rem(ix + gx_n - 1, gx_n)
    has_north, has_south = iy < gy_n - 1, iy > 0
    down = z < half
    step = jnp.where(down, 1, -1)
    first = jnp.where(down, 0, levels - 1)
    final = jnp.where(down, levels - 1, 0)
    has_out = (z > 0) & (z < gz_n - 1)
    mid = (z == half - 1) | (z == half)
    base = z * levels

    loads = [pltpu.make_async_copy(state.at[f], st.at[f], st_sem.at[f]) for f in range(4)]
    for copy in loads:
        copy.start()
    load_dep = pltpu.make_async_copy(dep_any, dep_ref, dep_sem)
    load_dep.start()
    load_mx = pltpu.make_async_copy(mixing, mx, mx_sem)
    load_mx.start()
    load_wind = pltpu.make_async_copy(wind_any, wind_ref, wind_sem)
    load_wind.start()

    barrier = pltpu.get_barrier_semaphore()
    for other in (east, west):
        pl.semaphore_signal(barrier, inc=1, device_id={"gx": other}, device_id_type=MESH)
    for d in range(1, gz_n):
        pl.semaphore_signal(barrier, inc=1, device_id={"gz": lax.rem(z + d, gz_n)}, device_id_type=MESH)

    @pl.when(has_north)
    def _():
        pl.semaphore_signal(barrier, inc=1, device_id={"gy": iy + 1}, device_id_type=MESH)

    @pl.when(has_south)
    def _():
        pl.semaphore_signal(barrier, inc=1, device_id={"gy": iy - 1}, device_id_type=MESH)

    greeted = 2 + (gz_n - 1) + jnp.where(has_north, 1, 0) + jnp.where(has_south, 1, 0)

    def remote(src, dst, send, recv, **device):
        return pltpu.make_async_remote_copy(
            src_ref=src, dst_ref=dst, send_sem=send, recv_sem=recv, device_id=device, device_id_type=MESH
        )

    lane = lax.broadcasted_iota(jnp.int32, (cols, 128), 1)

    part = levels // 2

    def rows_out(ch):
        def one(i, carry):
            k = first + step * (ch * part + i)
            for f in range(3):
                hx_src[0, ch, f, pl.ds(i, 1), :] = st[f, k, cols - 1:cols, :]
                hx_src[1, ch, f, pl.ds(i, 1), :] = st[f, k, 0:1, :]
            return carry

        lax.fori_loop(0, part, one, 0)

    x_copies = [
        [
            remote(hx_src.at[0, ch], hx.at[0, ch], hx_send.at[0, ch], hx_recv.at[0, ch], gx=east),
            remote(hx_src.at[1, ch], hx.at[1, ch], hx_send.at[1, ch], hx_recv.at[1, ch], gx=west),
        ]
        for ch in range(2)
    ]
    v_copies = [
        remote(hv_src.at[0], hv.at[0], hv_send.at[0], hv_recv.at[0], gx=east),
        remote(hv_src.at[1], hv.at[1], hv_send.at[1], hv_recv.at[1], gx=west),
    ]
    for copy in loads[:3]:
        copy.wait()
    rows_out(0)
    pl.semaphore_wait(barrier, greeted)
    for copy in x_copies[0]:
        copy.start()

    def mixing_copy(target):
        return remote(mixing.at[:, levels - 1], mh, m_send, m_recv, gz=target)

    sends_mixing = (z >= half) & (z < gz_n - 1)

    @pl.when(sends_mixing)
    def _():
        mixing_copy(z + 1).start()

    loads[3].wait()

    y_copies = [
        remote(hy_src.at[0], hy.at[0], hy_send.at[0], hy_recv.at[0], gy=lax.rem(iy + 1, gy_n)),
        remote(hy_src.at[1], hy.at[1], hy_send.at[1], hy_recv.at[1], gy=lax.rem(iy + gy_n - 1, gy_n)),
    ]
    zero = jnp.zeros((cols, 128), F32)

    def pack(side):
        def one(k, packed):
            shift = k + 1 if side == 0 else k
            lanes = pl.ds(rows - 128, 128) if side == 0 else pl.ds(0, 128)
            return tuple(
                jnp.where(lane == k, pltpu.roll(st[f, k, :, lanes], shift, 1), packed[f]) for f in range(4)
            )

        packed = lax.fori_loop(0, levels, one, (zero,) * 4)
        for f in range(4):
            hy_src[side, f] = packed[f]

    for side, present, absent_in in ((0, has_north, 1), (1, has_south, 0)):

        @pl.when(present)
        def _(side=side):
            pack(side)
            y_copies[side].start()

        @pl.when(jnp.logical_not(present))
        def _(side=side, absent_in=absent_in):
            for f in range(4):
                hy_src[side, f] = zero
                hy[absent_in, f] = zero

    rows_out(1)
    for copy in x_copies[1]:
        copy.start()

    def v_rows(k, carry):
        hv_src[0, pl.ds(k, 1), :] = st[3, k, cols - 1:cols, :]
        hv_src[1, pl.ds(k, 1), :] = st[3, k, 0:1, :]
        return carry

    lax.fori_loop(0, levels, v_rows, 0)
    for copy in v_copies:
        copy.start()

    load_dep.wait()
    start_x = pl.multiple_of(ix * cols, cols)
    start_y = pl.multiple_of(iy * rows, rows)
    dep = dep_ref[pl.ds(start_x, cols), pl.ds(start_y, rows)]
    dep_w = dep_ref[pl.ds(lax.rem(start_x + total_x - 1, total_x), 1), pl.ds(start_y, rows)]
    dep_e = dep_ref[pl.ds(lax.rem(start_x + cols, total_x), 1), pl.ds(start_y, rows)]
    block_s = pl.multiple_of(lax.rem(start_y + total_y - 128, total_y), 128)
    block_n = pl.multiple_of(lax.rem(start_y + rows, total_y), 128)
    dep_s = dep_ref[pl.ds(start_x, cols), pl.ds(block_s, 128)][:, 127:128]
    dep_n = dep_ref[pl.ds(start_x, cols), pl.ds(block_n, 128)][:, 0:1]
    dep_s = jnp.where(has_south, dep_s, 0)
    dep_n = jnp.where(has_north, dep_n, 0)

    tile_row = lax.broadcasted_iota(jnp.int32, (8, rows), 0)
    tiles = cols // 8

    def from_east(array, row):
        turned = [pltpu.roll(array[8 * i:8 * i + 8], 7, 0) for i in range(tiles)] + [row]
        return jnp.concatenate([jnp.where(tile_row == 7, turned[i + 1], turned[i]) for i in range(tiles)], axis=0)

    def from_west(array, row):
        turned = [row] + [pltpu.roll(array[8 * i:8 * i + 8], 1, 0) for i in range(tiles)]
        return jnp.concatenate([jnp.where(tile_row == 0, turned[i], turned[i + 1]) for i in range(tiles)], axis=0)

    def from_north(array, block):
        turned = [pltpu.roll(array[:, 128 * b:128 * b + 128], 127, 1) for b in range(blocks)] + [block]
        return jnp.concatenate([jnp.where(lane == 127, turned[b + 1], turned[b]) for b in range(blocks)], axis=1)

    def from_south(array, block):
        turned = [block] + [pltpu.roll(array[:, 128 * b:128 * b + 128], 1, 1) for b in range(blocks)]
        return jnp.concatenate([jnp.where(lane == 0, turned[b], turned[b + 1]) for b in range(blocks)], axis=1)

    least_e = jnp.minimum(dep, from_east(dep, dep_e))
    least_n = jnp.minimum(dep, from_north(dep, jnp.broadcast_to(dep_n, (cols, 128))))
    least_w = jnp.minimum(dep[0:1], dep_w)
    depths[0], depths[1], depths[2] = dep, least_e, least_n

    def total_one(k, total):
        return total + density_of(st[0, k], st[1, k]) * as_float(base + k < dep)

    s_src[...] = lax.fori_loop(0, levels, total_one, jnp.zeros((cols, rows), F32))

    def s_copy(d, slot):
        return remote(s_src, s_in.at[slot], s_send.at[d - 1], s_recv.at[slot], gz=lax.rem(z + d, gz_n))

    def h_copy(d, slot):
        return remote(h_src, h_in.at[slot], h_send.at[d - 1], h_recv.at[slot], gz=lax.rem(z + d, gz_n))

    for d in range(1, gz_n):

        @pl.when(z + d < gz_n)
        def _(d=d):
            s_copy(d, z).start()

    load_mx.wait()
    slot_in = jnp.where(mid, 1, 0)
    inward = jnp.clip(z + step, 0, gz_n - 1)
    outward = jnp.clip(z - step, 0, gz_n - 1)
    other_z = lax.rem(z + 1, gz_n)
    c_copy = remote(c_out, c_in.at[slot_in], c_send, c_recv.at[slot_in], gz=inward)

    def below(m):
        return mx[m, levels - 1] * as_float(base + levels < dep)

    def coefficients():
        def coefficient(t, carry):
            k = first + step * t
            ci = jnp.where(down, k, k - 1)
            wet = as_float(base + ci + 1 < dep)
            new = []
            for m in range(2):
                c = mx[m, ci] * wet
                over = 1.0 / (carry[m] + c)
                ratio = c * over
                rat[m, k + step] = ratio
                inv[m, k] = over
                new.append(1.0 + ratio * carry[m])
            via[k] = over * carry[2]
            new.append(ratio * carry[2])
            return tuple(new)

        carry = lax.fori_loop(0, levels - 1, coefficient, (d_last[0], d_last[1], w_last[...]))
        for m in range(2):
            d_last[m] = carry[m]
            rat[m, first] = jnp.zeros((cols, rows), F32)
        w_last[...] = carry[2]

        @pl.when(down)
        def _():
            for m in range(2):
                c = below(m)
                ratio = c / (d_last[m] + c)
                k_out[m] = ratio
                c_out[m] = ratio * d_last[m]

        @pl.when(jnp.logical_not(down))
        def _():
            for m in range(2):
                k_out[m] = jnp.ones((cols, rows), F32)
                c_out[m] = d_last[m]

        c_copy.start()

    @pl.when(jnp.logical_not(has_out))
    def _():
        for m in range(2):
            d_last[m] = jnp.ones((cols, rows), F32)
            r_in[0, 2 + m] = jnp.zeros((cols, rows), F32)
        w_last[...] = jnp.zeros((cols, rows), F32)
        coefficients()

    for copy in x_copies[0]:
        copy.wait_recv()

    @pl.when(has_south)
    def _():
        y_copies[0].wait_recv()

    @pl.when(has_north)
    def _():
        y_copies[1].wait_recv()

    lane_level = jnp.where(lane < levels, base + lane, 1 << 20)

    wet_s = lane_level < jnp.minimum(dep_s, dep[:, 0:1])

    def takes(both, wet):
        vel = both * jnp.where(wet, 0.125, 0.0).astype(F32)
        near = jnp.maximum(vel, 0.0) + jnp.where(wet, 0.08, 0.0).astype(F32)
        return near, vel - near

    take_s, take_n = takes(hy[0, 3] + hy_src[1, 3], wet_s)
    for f in range(4):
        south_flux[f] = take_s * hy[0, f] + take_n * hy_src[1, f]

    spans = [slice(8 * i, 8 * i + 8) for i in range(tiles)]
    tile_lane = lax.broadcasted_iota(jnp.int32, (8, 128), 1)

    def halves(array):
        return [array[:, 128 * b:128 * b + 128] for b in range(blocks)]

    def tile_north(array, block):
        turned = [pltpu.roll(a, 127, 1) for a in halves(array)] + [block]
        return jnp.concatenate([jnp.where(tile_lane == 127, turned[b + 1], turned[b]) for b in range(blocks)], axis=1)

    def tile_south(array, block):
        turned = [block] + [pltpu.roll(a, 1, 1) for a in halves(array)]
        return jnp.concatenate([jnp.where(tile_lane == 0, turned[b], turned[b + 1]) for b in range(blocks)], axis=1)

    class Easts:
        def __init__(self, get, row):
            self.get, self.row = get, row
            self.ahead = get(0)
            self.turned = pltpu.roll(self.ahead, 7, 0)

        def next(self, i):
            here, turned = self.ahead, self.turned
            if i + 1 < tiles:
                self.ahead = self.get(i + 1)
                self.turned = pltpu.roll(self.ahead, 7, 0)
            else:
                self.turned = self.row
            return here, jnp.where(tile_row == 7, self.turned, turned)

    class Wests:
        def __init__(self, row):
            self.turned = row

        def next(self, tile):
            before, self.turned = self.turned, pltpu.roll(tile, 1, 0)
            return jnp.where(tile_row == 0, before, self.turned)

    def moved_of(f, i, c, c_e, wests, to_north, to_south, ax, bx, ay, by):
        c_n = tile_north(c, pltpu.roll(hy[1, f, spans[i]], to_north, 1))
        flux_x = ax * c + bx * c_e
        flux_y = ay * c + by * c_n
        flux_w = wests.next(flux_x)
        flux_s = tile_south(flux_y, pltpu.roll(south_flux[f, spans[i]], to_south, 1))
        return c - (flux_x - flux_w + flux_y - flux_s)

    def advance_tracers(t, carry, ch):
        k = first + step * t
        ct = pl.ds(t - ch * part, 1)
        kg = base + k
        at = pl.ds(k, 1)
        to_north, to_south = 127 - k, lax.rem(128 - k, 128)
        aw, bw = takes(hx[0, ch, 2, ct, :] + st[2, k, 0:1, :], kg < least_w)
        take_w[0, at, :], take_w[1, at, :] = aw, bw
        east_of = [Easts(lambda i, f=f: st[f, k, spans[i], :], hx[1, ch, f, ct, :]) for f in range(3)]
        west_of = [Wests(aw * hx[0, ch, f, ct, :] + bw * st[f, k, 0:1, :]) for f in range(2)]
        for i in range(tiles):
            sp = spans[i]
            u, u_e = east_of[2].next(i)
            v = st[3, k, sp, :]
            ax, bx = takes(u + u_e, kg < depths[1, sp])
            ay, by = takes(v + tile_north(v, pltpu.roll(hy[1, 3, sp], to_north, 1)), kg < depths[2, sp])
            take[0, k, sp, :], take[1, k, sp, :], take[2, k, sp, :], take[3, k, sp, :] = ax, bx, ay, by
            wet = as_float(kg < depths[0, sp])
            for f in range(2):
                c, c_e = east_of[f].next(i)
                fr[f, k, sp, :] = moved_of(f, i, c, c_e, west_of[f], to_north, to_south, ax, bx, ay, by) * wet
        return carry

    lax.fori_loop(0, part, functools.partial(advance_tracers, ch=0), 0)

    for copy in x_copies[1]:
        copy.wait_recv()

    def where_rows(t):
        ch = jnp.where(t < part, 0, 1)
        return ch, pl.ds(t - ch * part, 1)

    def total_rows(t, totals):
        ch, at = where_rows(t)
        k = first + step * t
        w = density_of(hx[0, ch, 0, at, :], hx[0, ch, 1, at, :]) * as_float(base + k < dep_w)
        e = density_of(hx[1, ch, 0, at, :], hx[1, ch, 1, at, :]) * as_float(base + k < dep_e)
        return totals[0] + w, totals[1] + e

    row_zero = jnp.zeros((1, rows), F32)
    tot_w, tot_e = lax.fori_loop(0, levels, total_rows, (row_zero, row_zero))

    def running(dens):
        sh = 1
        while sh < levels:
            dens = dens + jnp.where(lane >= sh, pltpu.roll(dens, sh, 1), 0.0)
            sh *= 2
        return dens

    dens_n = density_of(hy[1, 0], hy[1, 1]) * as_float(lane_level < dep_n)
    dens_s = density_of(hy[0, 0], hy[0, 1]) * as_float(lane_level < dep_s)
    dens_o = density_of(hy_src[1, 0], hy_src[1, 1]) * as_float(lane_level < dep[:, 0:1])
    tot_n = jnp.sum(dens_n, axis=1, keepdims=True)
    tot_s = jnp.sum(dens_s, axis=1, keepdims=True)
    h_src[0:cols, :] = jnp.where(lane == 0, tot_s, jnp.where(lane == 1, tot_n, 0.0))
    for b in range(blocks):
        piece = slice(b * 128, b * 128 + 128)
        at = cols + 8 * b
        h_src[at:at + 8, :] = jnp.concatenate([tot_w[:, piece], tot_e[:, piece], jnp.zeros((6, 128), F32)], axis=0)

    for d in range(1, gz_n):

        @pl.when(z + d < gz_n)
        def _(d=d):
            h_copy(d, z).start()

    lax.fori_loop(part, levels, functools.partial(advance_tracers, ch=1), 0)

    @pl.when(has_out)
    def _():
        remote(c_out, c_in.at[0], c_send, c_recv.at[0], gz=other_z).wait_recv()

        @pl.when(down)
        def _():
            for m in range(2):
                k_in[m] = jnp.ones((cols, rows), F32)
                d_last[m] = 1.0 + c_in[0, m]

        @pl.when(jnp.logical_not(down))
        def _():
            for m in range(2):
                c = below(m)
                ratio = c / (c_in[0, m] + c)
                k_in[m] = ratio
                d_last[m] = 1.0 + ratio * c_in[0, m]

        w_last[...] = k_in[1]
        coefficients()

    in_copies = [remote(h_out.at[f], r_in.at[slot_in, f], r_send.at[f], r_recv.at[slot_in, f], gz=inward) for f in range(4)]
    out_copies = [remote(fr.at[f, first], r_in.at[1, f], x_send.at[f], r_recv.at[1, f], gz=outward) for f in range(4)]
    stores = [pltpu.make_async_copy(fr.at[f], out.at[f], out_sem.at[f]) for f in range(4)]

    def wait_in(slot, f):
        remote(h_out.at[f], r_in.at[slot, f], r_send.at[f], r_recv.at[slot, f], gz=other_z).wait_recv()

    @pl.when(has_out)
    def _():
        for f in range(2):
            wait_in(0, f)
            fr[f, first] = fr[f, first] + k_in[0] * r_in[0, f]

    def forward(t, g):
        k = first + step * t
        ratio = rat[0, k]
        new = tuple(fr[f, k] + ratio * g[f] for f in range(2))
        for f in range(2):
            fr[f, k] = new[f]
        return new

    g = lax.fori_loop(1, levels, forward, (fr[0, first], fr[1, first]))
    for f in range(2):
        h_out[f] = k_out[0] * g[f]
        in_copies[f].start()

    s_acc[...] = jnp.zeros_like(s_acc)
    h_acc[...] = jnp.zeros_like(h_acc)
    for p in range(gz_n - 1):

        @pl.when(z > p)
        def _(p=p):
            s_copy(1, p).wait_recv()
            s_acc[...] = s_acc[...] + s_in[p]
            h_copy(1, p).wait_recv()
            h_acc[...] = h_acc[...] + h_in[p]

    edge_p[0] = h_acc[0:cols, 1:2] + running(dens_n) - 0.5 * dens_n
    p_s = h_acc[0:cols, 0:1] + running(dens_s) - 0.5 * dens_s
    p_o = s_acc[:, 0:1] + running(dens_o) - 0.5 * dens_o
    edge_p[1] = as_float(wet_s) * (p_o - p_s)

    sign = jnp.where(down, 1.0, -1.0).astype(F32)
    own = jnp.where(down, 0.0, 1.0).astype(F32)

    def wide_row(ref, r):
        return jnp.concatenate([ref[cols + 8 * b + r:cols + 8 * b + r + 1, :] for b in range(blocks)], axis=1)

    run_ref[...] = s_acc[...] + own * s_src[...]
    g_ref[...] = jnp.zeros_like(g_ref)
    run_w = wide_row(h_acc, 0) + own * wide_row(h_src, 0)
    run_e = wide_row(h_acc, 1) + own * wide_row(h_src, 1)
    row_lane = lax.broadcasted_iota(jnp.int32, (8, rows), 1)
    coriolis = 0.3 * (0.5 + ((start_y + row_lane).astype(F32) + 0.5) / total_y)
    load_wind.wait()
    for copy in v_copies:
        copy.wait_recv()

    def advance(t, carry):
        run_w, run_e = carry
        k = first + step * t
        kg = base + k
        at = pl.ds(k, 1)
        to_north, to_south = 127 - k, lax.rem(128 - k, 128)
        ch, ct = where_rows(t)
        w = [hx[0, ch, f, ct, :] for f in range(3)] + [hv[0, at, :]]
        e = [hx[1, ch, f, ct, :] for f in range(3)] + [hv[1, at, :]]
        aw, bw = take_w[0, at, :], take_w[1, at, :]
        dens_w = density_of(w[0], w[1]) * as_float(kg < dep_w)
        dens_e = density_of(e[0], e[1]) * as_float(kg < dep_e)
        p_w = run_w + (0.5 * sign) * dens_w
        p_e = run_e + (0.5 * sign) * dens_e
        top = jnp.where(kg == 0, 1.0, 0.0).astype(F32)

        def pressure(i):
            sp = spans[i]
            dens = density_of(st[0, k, sp, :], st[1, k, sp, :]) * as_float(kg < depths[0, sp])
            run = run_ref[sp, :]
            run_ref[sp, :] = run + sign * dens
            return run + (0.5 * sign) * dens

        east_p = Easts(pressure, p_e)
        west_p = Wests(as_float(kg < least_w) * (east_p.ahead[0:1] - p_w))
        east_of = [Easts(lambda i, f=f: st[f, k, spans[i], :], e[f]) for f in (2, 3)]
        west_of = [Wests(aw * w[f] + bw * st[f, k, 0:1, :]) for f in (2, 3)]
        for i in range(tiles):
            sp = spans[i]
            coefs = [take[n, k, sp, :] for n in range(4)]
            wet = as_float(kg < depths[0, sp])
            p, p_east = east_p.next(i)
            g_x = as_float(kg < depths[1, sp]) * (p_east - p)
            g_y = as_float(kg < depths[2, sp]) * (tile_north(p, pltpu.roll(edge_p[0, sp], to_north, 1)) - p)
            g_x = g_x + west_p.next(g_x)
            g_y = g_y + tile_south(g_y, pltpu.roll(edge_p[1, sp], to_south, 1))
            (u, u_e), (v, v_e) = east_of[0].next(i), east_of[1].next(i)
            ratio = rat[1, k, sp, :]
            new_u = moved_of(2, i, u, u_e, west_of[0], to_north, to_south, *coefs)
            new_u = (new_u + coriolis * v - 0.015 * g_x + top * wind_ref[0, sp, :]) * wet + ratio * g_ref[0, sp, :]
            g_ref[0, sp, :] = new_u
            fr[2, k, sp, :] = new_u
            new_v = moved_of(3, i, v, v_e, west_of[1], to_north, to_south, *coefs)
            new_v = (new_v - coriolis * u - 0.015 * g_y + top * wind_ref[1, sp, :]) * wet + ratio * g_ref[1, sp, :]
            g_ref[1, sp, :] = new_v
            fr[3, k, sp, :] = new_v
        return run_w + sign * dens_w, run_e + sign * dens_e

    lax.fori_loop(0, levels, advance, (run_w, run_e))

    @pl.when(mid)
    def _():
        remote(c_out, c_in.at[1], c_send, c_recv.at[1], gz=other_z).wait_recv()

    receives_mixing = z > half

    @pl.when(receives_mixing)
    def _():
        mixing_copy(other_z).wait_recv()

    for m in range(2):

        @pl.when(down & jnp.logical_not(mid))
        def _(m=m):
            c = below(m)
            over = 1.0 / (d_last[m] + c)
            k_a[m] = over
            k_b[m] = c * over

        @pl.when(receives_mixing)
        def _(m=m):
            c = mh[m] * as_float(base < dep)
            over = 1.0 / (d_last[m] + c)
            k_a[m] = over
            k_b[m] = c * over

        @pl.when(z == half - 1)
        def _(m=m):
            c = below(m)
            ratio = c / (c_in[1, m] + c)
            over = 1.0 / (d_last[m] + ratio * c_in[1, m])
            k_a[m] = over
            k_b[m] = ratio * over

        @pl.when(z == half)
        def _(m=m):
            over = 1.0 / (d_last[m] + c_in[1, m])
            k_a[m] = over
            k_b[m] = over

    def backward_tracers():
        for f in range(2):
            wait_in(1, f)
            fr[f, final] = k_a[0] * fr[f, final] + k_b[0] * r_in[1, f]

        def backward(t, x):
            k = final - step * t
            ratio, over = rat[0, k + step], inv[0, k]
            new = tuple(over * fr[f, k] + ratio * x[f] for f in range(2))
            for f in range(2):
                fr[f, k] = new[f]
            return new

        lax.fori_loop(1, levels, backward, (fr[0, final], fr[1, final]))
        for f in range(2):

            @pl.when(has_out)
            def _(f=f):
                out_copies[f].start()

            stores[f].start()

    @pl.when(has_out)
    def _():
        backward_tracers()

    for f in (2, 3):

        @pl.when(has_out)
        def _(f=f):
            wait_in(0, f)
            fr[f, final] = fr[f, final] + w_last[...] * r_in[0, f]

        h_out[f] = k_out[1] * fr[f, final]
        in_copies[f].start()

    @pl.when(jnp.logical_not(has_out))
    def _():
        backward_tracers()

    for f in (2, 3):
        wait_in(1, f)
        came = r_in[0, f]
        x = k_a[1] * fr[f, final] + k_b[1] * r_in[1, f]
        fr[f, final] = x

        def backward(t, x, f=f, came=came):
            k = final - step * t
            x = inv[1, k] * fr[f, k] + rat[1, k + step] * x + via[k] * came
            fr[f, k] = x
            return x

        lax.fori_loop(1, levels, backward, x)

        @pl.when(has_out)
        def _(f=f):
            out_copies[f].start()

        stores[f].start()

    for copy in x_copies[0] + x_copies[1] + v_copies:
        copy.wait_send()
    for side, present in ((0, has_north), (1, has_south)):

        @pl.when(present)
        def _(side=side):
            y_copies[side].wait_send()

    for d in range(1, gz_n):

        @pl.when(z + d < gz_n)
        def _(d=d):
            s_copy(d, z).wait_send()
            h_copy(d, z).wait_send()

    @pl.when(sends_mixing)
    def _():
        mixing_copy(z + 1).wait_send()

    c_copy.wait_send()
    for f in range(4):
        in_copies[f].wait_send()

        @pl.when(has_out)
        def _(f=f):
            out_copies[f].wait_send()

        stores[f].wait()


def place(source, target, held, in_sem, out_sem):
    part = source.shape[1] // 2
    pieces = [(f, h) for f in range(4) for h in range(2)]
    ins = [
        pltpu.make_async_copy(source.at[f, pl.ds(h * part, part)], held.at[f, pl.ds(h * part, part)], in_sem.at[f, h])
        for f, h in pieces
    ]
    outs = [
        pltpu.make_async_copy(held.at[f, pl.ds(h * part, part)], target.at[f, pl.ds(h * part, part)], out_sem.at[f, h])
        for f, h in pieces
    ]
    for copy in ins:
        copy.start()
    for arrived, leaving in zip(ins, outs):
        arrived.wait()
        leaving.start()
    for copy in outs:
        copy.wait()


def per_device(sizes, state, mixing, depth_levels, wind):
    _, levels, cols, rows = state.shape
    gz_n = sizes[2]
    blocks = rows // 128
    any_spec = pl.BlockSpec(memory_space=pl.ANY)
    vmem = lambda *shape: pltpu.VMEM(shape, F32)
    dma = lambda *shape: pltpu.SemaphoreType.DMA(shape)
    tile = (cols, rows)
    earlier = max(gz_n - 1, 1)
    h_rows = cols + 8 * blocks
    one = pltpu.SemaphoreType.DMA
    scratch = [
        pltpu.VMEM(depth_levels.shape, jnp.int32), vmem(2, *tile),
        vmem(4, levels, *tile), vmem(2, levels, *tile), vmem(4, levels, *tile),
        vmem(2, levels, *tile), vmem(2, levels, *tile),
        vmem(4, levels, *tile), vmem(2, levels, rows), vmem(levels, *tile), vmem(*tile),
        pltpu.VMEM((3, *tile), jnp.int32), vmem(*tile), vmem(2, *tile),
        vmem(2, 2, 3, levels // 2, rows), vmem(2, 2, 3, levels // 2, rows), vmem(2, levels, rows), vmem(2, levels, rows),
        vmem(2, 4, cols, 128), vmem(2, 4, cols, 128),
        vmem(4, cols, 128), vmem(2, cols, 128),
        vmem(*tile), vmem(earlier, *tile), vmem(*tile),
        vmem(h_rows, 128), vmem(earlier, h_rows, 128), vmem(h_rows, 128),
        vmem(2, *tile), vmem(2, 2, *tile), vmem(2, *tile), vmem(4, *tile), vmem(2, 4, *tile),
        vmem(2, *tile), vmem(2, *tile), vmem(2, *tile), vmem(2, *tile), vmem(2, *tile),
        one, one, dma(4), one, dma(4), dma(2, 2), dma(2, 2), dma(2), dma(2), dma(2), dma(2),
        dma(earlier), dma(earlier), dma(earlier), dma(earlier), one, dma(2), one, one, dma(4), dma(2, 4), dma(4),
    ]
    solved = pl.pallas_call(
        functools.partial(kernel, sizes),
        out_shape=jax.ShapeDtypeStruct(state.shape, F32),
        in_specs=[any_spec] * 4,
        out_specs=any_spec,
        scratch_shapes=scratch,
        compiler_params=pltpu.CompilerParams(
            collective_id=0, has_side_effects=True, vmem_limit_bytes=60 * 1024 * 1024
        ),
        cost_estimate=pl.CostEstimate(flops=state.size * 60, bytes_accessed=state.size * 10, transcendentals=0),
    )(state, mixing, depth_levels, wind)
    return pl.pallas_call(
        place,
        out_shape=jax.ShapeDtypeStruct(state.shape, F32),
        in_specs=[any_spec],
        out_specs=any_spec,
        scratch_shapes=[vmem(*state.shape), dma(4, 2), dma(4, 2)],
        compiler_params=pltpu.CompilerParams(vmem_limit_bytes=60 * 1024 * 1024),
        cost_estimate=pl.CostEstimate(flops=0, bytes_accessed=state.size * 8, transcendentals=0),
    )(solved)


def solution(mesh):
    sizes = tuple(mesh.shape[name] for name in ("gx", "gy", "gz"))
    return jax.shard_map(
        functools.partial(per_device, sizes),
        mesh=mesh,
        in_specs=(P(None, "gz", "gx", "gy"), P(None, "gz", "gx", "gy"), P(), P(None, "gx", "gy")),
        out_specs=P(None, "gz", "gx", "gy"),
        check_vma=False,
    )
```

```python
import functools

import jax
import jax.numpy as jnp
from jax import lax
from jax.experimental import pallas as pl
from jax.experimental.pallas import tpu as pltpu
from jax.sharding import PartitionSpec as P

MESH = pl.DeviceIdType.MESH
F32 = jnp.float32


def density_of(t, s):
    return t * (-0.3 - 0.05 * t) + 0.7 * s


def as_float(mask):
    return jnp.where(mask, 1.0, 0.0).astype(F32)


def kernel(
    sizes, state, mixing, dep_any, wind_any, out,
    dep_ref, wind_ref, st, mx, fr, rat, inv, take, take_w, via, w_last, depths, run_ref, g_ref, hx_src, hx, hv_src, hv, hy_src, hy, south_flux, edge_p,
    s_src, s_in, s_acc, h_src, h_in, h_acc,
    c_out, c_in, mh, h_out, r_in, k_in, k_out, k_a, k_b, d_last,
    dep_sem, wind_sem, st_sem, mx_sem, out_sem, hx_send, hx_recv, hv_send, hv_recv, hy_send, hy_recv,
    s_send, s_recv, h_send, h_recv, c_send, c_recv, m_send, m_recv, r_send, r_recv, x_send,
):
    gx_n, gy_n, gz_n = sizes
    _, levels, cols, rows = st.shape
    total_x, total_y = dep_any.shape
    blocks = rows // 128
    half = gz_n // 2
    ix, iy, z = lax.axis_index("gx"), lax.axis_index("gy"), lax.axis_index("gz")
    east, west = lax.rem(ix + 1, gx_n), lax.rem(ix + gx_n - 1, gx_n)
    has_north, has_south = iy < gy_n - 1, iy > 0
    down = z < half
    step = jnp.where(down, 1, -1)
    first = jnp.where(down, 0, levels - 1)
    final = jnp.where(down, levels - 1, 0)
    has_out = (z > 0) & (z < gz_n - 1)
    mid = (z == half - 1) | (z == half)
    base = z * levels

    loads = [pltpu.make_async_copy(state.at[f], st.at[f], st_sem.at[f]) for f in range(4)]
    for copy in loads:
        copy.start()
    load_dep = pltpu.make_async_copy(dep_any, dep_ref, dep_sem)
    load_dep.start()
    load_mx = pltpu.make_async_copy(mixing, mx, mx_sem)
    load_mx.start()
    load_wind = pltpu.make_async_copy(wind_any, wind_ref, wind_sem)
    load_wind.start()

    barrier = pltpu.get_barrier_semaphore()
    for other in (east, west):
        pl.semaphore_signal(barrier, inc=1, device_id={"gx": other}, device_id_type=MESH)
    for d in range(1, gz_n):
        pl.semaphore_signal(barrier, inc=1, device_id={"gz": lax.rem(z + d, gz_n)}, device_id_type=MESH)

    @pl.when(has_north)
    def _():
        pl.semaphore_signal(barrier, inc=1, device_id={"gy": iy + 1}, device_id_type=MESH)

    @pl.when(has_south)
    def _():
        pl.semaphore_signal(barrier, inc=1, device_id={"gy": iy - 1}, device_id_type=MESH)

    greeted = 2 + (gz_n - 1) + jnp.where(has_north, 1, 0) + jnp.where(has_south, 1, 0)

    def remote(src, dst, send, recv, **device):
        return pltpu.make_async_remote_copy(
            src_ref=src, dst_ref=dst, send_sem=send, recv_sem=recv, device_id=device, device_id_type=MESH
        )

    lane = lax.broadcasted_iota(jnp.int32, (cols, 128), 1)

    part = levels // 2

    def rows_out(ch):
        def one(i, carry):
            k = first + step * (ch * part + i)
            for f in range(3):
                hx_src[0, ch, f, pl.ds(i, 1), :] = st[f, k, cols - 1:cols, :]
                hx_src[1, ch, f, pl.ds(i, 1), :] = st[f, k, 0:1, :]
            return carry

        lax.fori_loop(0, part, one, 0)

    x_copies = [
        [
            remote(hx_src.at[0, ch], hx.at[0, ch], hx_send.at[0, ch], hx_recv.at[0, ch], gx=east),
            remote(hx_src.at[1, ch], hx.at[1, ch], hx_send.at[1, ch], hx_recv.at[1, ch], gx=west),
        ]
        for ch in range(2)
    ]
    v_copies = [
        remote(hv_src.at[0], hv.at[0], hv_send.at[0], hv_recv.at[0], gx=east),
        remote(hv_src.at[1], hv.at[1], hv_send.at[1], hv_recv.at[1], gx=west),
    ]
    for copy in loads[:3]:
        copy.wait()
    rows_out(0)
    pl.semaphore_wait(barrier, greeted)
    for copy in x_copies[0]:
        copy.start()

    def mixing_copy(target):
        return remote(mixing.at[:, levels - 1], mh, m_send, m_recv, gz=target)

    sends_mixing = (z >= half) & (z < gz_n - 1)

    @pl.when(sends_mixing)
    def _():
        mixing_copy(z + 1).start()

    loads[3].wait()

    y_copies = [
        remote(hy_src.at[0], hy.at[0], hy_send.at[0], hy_recv.at[0], gy=lax.rem(iy + 1, gy_n)),
        remote(hy_src.at[1], hy.at[1], hy_send.at[1], hy_recv.at[1], gy=lax.rem(iy + gy_n - 1, gy_n)),
    ]
    zero = jnp.zeros((cols, 128), F32)

    def pack(side):
        def one(k, packed):
            shift = k + 1 if side == 0 else k
            lanes = pl.ds(rows - 128, 128) if side == 0 else pl.ds(0, 128)
            return tuple(
                jnp.where(lane == k, pltpu.roll(st[f, k, :, lanes], shift, 1), packed[f]) for f in range(4)
            )

        packed = lax.fori_loop(0, levels, one, (zero,) * 4)
        for f in range(4):
            hy_src[side, f] = packed[f]

    for side, present, absent_in in ((0, has_north, 1), (1, has_south, 0)):

        @pl.when(present)
        def _(side=side):
            pack(side)
            y_copies[side].start()

        @pl.when(jnp.logical_not(present))
        def _(side=side, absent_in=absent_in):
            for f in range(4):
                hy_src[side, f] = zero
                hy[absent_in, f] = zero

    rows_out(1)
    for copy in x_copies[1]:
        copy.start()

    def v_rows(k, carry):
        hv_src[0, pl.ds(k, 1), :] = st[3, k, cols - 1:cols, :]
        hv_src[1, pl.ds(k, 1), :] = st[3, k, 0:1, :]
        return carry

    lax.fori_loop(0, levels, v_rows, 0)
    for copy in v_copies:
        copy.start()

    load_dep.wait()
    start_x = pl.multiple_of(ix * cols, cols)
    start_y = pl.multiple_of(iy * rows, rows)
    dep = dep_ref[pl.ds(start_x, cols), pl.ds(start_y, rows)]
    dep_w = dep_ref[pl.ds(lax.rem(start_x + total_x - 1, total_x), 1), pl.ds(start_y, rows)]
    dep_e = dep_ref[pl.ds(lax.rem(start_x + cols, total_x), 1), pl.ds(start_y, rows)]
    block_s = pl.multiple_of(lax.rem(start_y + total_y - 128, total_y), 128)
    block_n = pl.multiple_of(lax.rem(start_y + rows, total_y), 128)
    dep_s = dep_ref[pl.ds(start_x, cols), pl.ds(block_s, 128)][:, 127:128]
    dep_n = dep_ref[pl.ds(start_x, cols), pl.ds(block_n, 128)][:, 0:1]
    dep_s = jnp.where(has_south, dep_s, 0)
    dep_n = jnp.where(has_north, dep_n, 0)

    tile_row = lax.broadcasted_iota(jnp.int32, (8, rows), 0)
    tiles = cols // 8

    def from_east(array, row):
        turned = [pltpu.roll(array[8 * i:8 * i + 8], 7, 0) for i in range(tiles)] + [row]
        return jnp.concatenate([jnp.where(tile_row == 7, turned[i + 1], turned[i]) for i in range(tiles)], axis=0)

    def from_west(array, row):
        turned = [row] + [pltpu.roll(array[8 * i:8 * i + 8], 1, 0) for i in range(tiles)]
        return jnp.concatenate([jnp.where(tile_row == 0, turned[i], turned[i + 1]) for i in range(tiles)], axis=0)

    def from_north(array, block):
        turned = [pltpu.roll(array[:, 128 * b:128 * b + 128], 127, 1) for b in range(blocks)] + [block]
        return jnp.concatenate([jnp.where(lane == 127, turned[b + 1], turned[b]) for b in range(blocks)], axis=1)

    def from_south(array, block):
        turned = [block] + [pltpu.roll(array[:, 128 * b:128 * b + 128], 1, 1) for b in range(blocks)]
        return jnp.concatenate([jnp.where(lane == 0, turned[b], turned[b + 1]) for b in range(blocks)], axis=1)

    least_e = jnp.minimum(dep, from_east(dep, dep_e))
    least_n = jnp.minimum(dep, from_north(dep, jnp.broadcast_to(dep_n, (cols, 128))))
    least_w = jnp.minimum(dep[0:1], dep_w)
    depths[0], depths[1], depths[2] = dep, least_e, least_n

    def total_one(k, total):
        return total + density_of(st[0, k], st[1, k]) * as_float(base + k < dep)

    s_src[...] = lax.fori_loop(0, levels, total_one, jnp.zeros((cols, rows), F32))

    def s_copy(d, slot):
        return remote(s_src, s_in.at[slot], s_send.at[d - 1], s_recv.at[slot], gz=lax.rem(z + d, gz_n))

    def h_copy(d, slot):
        return remote(h_src, h_in.at[slot], h_send.at[d - 1], h_recv.at[slot], gz=lax.rem(z + d, gz_n))

    for d in range(1, gz_n):

        @pl.when(z + d < gz_n)
        def _(d=d):
            s_copy(d, z).start()

    load_mx.wait()
    slot_in = jnp.where(mid, 1, 0)
    inward = jnp.clip(z + step, 0, gz_n - 1)
    outward = jnp.clip(z - step, 0, gz_n - 1)
    other_z = lax.rem(z + 1, gz_n)
    c_copy = remote(c_out, c_in.at[slot_in], c_send, c_recv.at[slot_in], gz=inward)

    def below(m):
        return mx[m, levels - 1] * as_float(base + levels < dep)

    def coefficients():
        def coefficient(t, carry):
            k = first + step * t
            ci = jnp.where(down, k, k - 1)
            wet = as_float(base + ci + 1 < dep)
            new = []
            for m in range(2):
                c = mx[m, ci] * wet
                over = 1.0 / (carry[m] + c)
                ratio = c * over
                rat[m, k + step] = ratio
                inv[m, k] = over
                new.append(1.0 + ratio * carry[m])
            via[k] = over * carry[2]
            new.append(ratio * carry[2])
            return tuple(new)

        carry = lax.fori_loop(0, levels - 1, coefficient, (d_last[0], d_last[1], w_last[...]))
        for m in range(2):
            d_last[m] = carry[m]
            rat[m, first] = jnp.zeros((cols, rows), F32)
        w_last[...] = carry[2]

        @pl.when(down)
        def _():
            for m in range(2):
                c = below(m)
                ratio = c / (d_last[m] + c)
                k_out[m] = ratio
                c_out[m] = ratio * d_last[m]

        @pl.when(jnp.logical_not(down))
        def _():
            for m in range(2):
                k_out[m] = jnp.ones((cols, rows), F32)
                c_out[m] = d_last[m]

        c_copy.start()

    @pl.when(jnp.logical_not(has_out))
    def _():
        for m in range(2):
            d_last[m] = jnp.ones((cols, rows), F32)
            r_in[0, 2 + m] = jnp.zeros((cols, rows), F32)
        w_last[...] = jnp.zeros((cols, rows), F32)
        coefficients()

    for copy in x_copies[0]:
        copy.wait_recv()

    @pl.when(has_south)
    def _():
        y_copies[0].wait_recv()

    @pl.when(has_north)
    def _():
        y_copies[1].wait_recv()

    lane_level = jnp.where(lane < levels, base + lane, 1 << 20)

    wet_s = lane_level < jnp.minimum(dep_s, dep[:, 0:1])

    def takes(both, wet):
        vel = both * jnp.where(wet, 0.125, 0.0).astype(F32)
        near = jnp.maximum(vel, 0.0) + jnp.where(wet, 0.08, 0.0).astype(F32)
        return near, vel - near

    take_s, take_n = takes(hy[0, 3] + hy_src[1, 3], wet_s)
    for f in range(4):
        south_flux[f] = take_s * hy[0, f] + take_n * hy_src[1, f]

    spans = [slice(8 * i, 8 * i + 8) for i in range(tiles)]
    tile_lane = lax.broadcasted_iota(jnp.int32, (8, 128), 1)

    def halves(array):
        return [array[:, 128 * b:128 * b + 128] for b in range(blocks)]

    def tile_north(array, block):
        turned = [pltpu.roll(a, 127, 1) for a in halves(array)] + [block]
        return jnp.concatenate([jnp.where(tile_lane == 127, turned[b + 1], turned[b]) for b in range(blocks)], axis=1)

    def tile_south(array, block):
        turned = [block] + [pltpu.roll(a, 1, 1) for a in halves(array)]
        return jnp.concatenate([jnp.where(tile_lane == 0, turned[b], turned[b + 1]) for b in range(blocks)], axis=1)

    class Easts:
        def __init__(self, get, row):
            self.get, self.row = get, row
            self.ahead = get(0)
            self.turned = pltpu.roll(self.ahead, 7, 0)

        def next(self, i):
            here, turned = self.ahead, self.turned
            if i + 1 < tiles:
                self.ahead = self.get(i + 1)
                self.turned = pltpu.roll(self.ahead, 7, 0)
            else:
                self.turned = self.row
            return here, jnp.where(tile_row == 7, self.turned, turned)

    class Wests:
        def __init__(self, row):
            self.turned = row

        def next(self, tile):
            before, self.turned = self.turned, pltpu.roll(tile, 1, 0)
            return jnp.where(tile_row == 0, before, self.turned)

    def moved_of(f, i, c, c_e, wests, to_north, to_south, ax, bx, ay, by):
        c_n = tile_north(c, pltpu.roll(hy[1, f, spans[i]], to_north, 1))
        flux_x = ax * c + bx * c_e
        flux_y = ay * c + by * c_n
        flux_w = wests.next(flux_x)
        flux_s = tile_south(flux_y, pltpu.roll(south_flux[f, spans[i]], to_south, 1))
        return c - (flux_x - flux_w + flux_y - flux_s)

    def advance_tracers(t, carry, ch):
        k = first + step * t
        ct = pl.ds(t - ch * part, 1)
        kg = base + k
        at = pl.ds(k, 1)
        to_north, to_south = 127 - k, lax.rem(128 - k, 128)
        aw, bw = takes(hx[0, ch, 2, ct, :] + st[2, k, 0:1, :], kg < least_w)
        take_w[0, at, :], take_w[1, at, :] = aw, bw
        east_of = [Easts(lambda i, f=f: st[f, k, spans[i], :], hx[1, ch, f, ct, :]) for f in range(3)]
        west_of = [Wests(aw * hx[0, ch, f, ct, :] + bw * st[f, k, 0:1, :]) for f in range(2)]
        for i in range(tiles):
            sp = spans[i]
            u, u_e = east_of[2].next(i)
            v = st[3, k, sp, :]
            ax, bx = takes(u + u_e, kg < depths[1, sp])
            ay, by = takes(v + tile_north(v, pltpu.roll(hy[1, 3, sp], to_north, 1)), kg < depths[2, sp])
            take[0, k, sp, :], take[1, k, sp, :], take[2, k, sp, :], take[3, k, sp, :] = ax, bx, ay, by
            wet = as_float(kg < depths[0, sp])
            for f in range(2):
                c, c_e = east_of[f].next(i)
                fr[f, k, sp, :] = moved_of(f, i, c, c_e, west_of[f], to_north, to_south, ax, bx, ay, by) * wet
        return carry

    lax.fori_loop(0, part, functools.partial(advance_tracers, ch=0), 0)

    for copy in x_copies[1]:
        copy.wait_recv()

    def where_rows(t):
        ch = jnp.where(t < part, 0, 1)
        return ch, pl.ds(t - ch * part, 1)

    def total_rows(t, totals):
        ch, at = where_rows(t)
        k = first + step * t
        w = density_of(hx[0, ch, 0, at, :], hx[0, ch, 1, at, :]) * as_float(base + k < dep_w)
        e = density_of(hx[1, ch, 0, at, :], hx[1, ch, 1, at, :]) * as_float(base + k < dep_e)
        return totals[0] + w, totals[1] + e

    row_zero = jnp.zeros((1, rows), F32)
    tot_w, tot_e = lax.fori_loop(0, levels, total_rows, (row_zero, row_zero))

    def running(dens):
        sh = 1
        while sh < levels:
            dens = dens + jnp.where(lane >= sh, pltpu.roll(dens, sh, 1), 0.0)
            sh *= 2
        return dens

    dens_n = density_of(hy[1, 0], hy[1, 1]) * as_float(lane_level < dep_n)
    dens_s = density_of(hy[0, 0], hy[0, 1]) * as_float(lane_level < dep_s)
    dens_o = density_of(hy_src[1, 0], hy_src[1, 1]) * as_float(lane_level < dep[:, 0:1])
    tot_n = jnp.sum(dens_n, axis=1, keepdims=True)
    tot_s = jnp.sum(dens_s, axis=1, keepdims=True)
    diagonal = lane == lax.broadcasted_iota(jnp.int32, (cols, 128), 0)

    def to_row(column):
        return jnp.sum(jnp.where(diagonal, column, 0.0), axis=0, keepdims=True)

    def to_column(row):
        return jnp.sum(jnp.where(diagonal, row, 0.0), axis=1, keepdims=True)

    pieces = [side[:, 128 * b:128 * b + 128] for side in (tot_w, tot_e) for b in range(blocks)]
    rest = jnp.zeros((h_src.shape[0] - 2 * blocks - 2, 128), F32)
    h_src[...] = jnp.concatenate(pieces + [to_row(tot_s), to_row(tot_n), rest], axis=0)

    for d in range(1, gz_n):

        @pl.when(z + d < gz_n)
        def _(d=d):
            h_copy(d, z).start()

    lax.fori_loop(part, levels, functools.partial(advance_tracers, ch=1), 0)

    @pl.when(has_out)
    def _():
        remote(c_out, c_in.at[0], c_send, c_recv.at[0], gz=other_z).wait_recv()

        @pl.when(down)
        def _():
            for m in range(2):
                k_in[m] = jnp.ones((cols, rows), F32)
                d_last[m] = 1.0 + c_in[0, m]

        @pl.when(jnp.logical_not(down))
        def _():
            for m in range(2):
                c = below(m)
                ratio = c / (c_in[0, m] + c)
                k_in[m] = ratio
                d_last[m] = 1.0 + ratio * c_in[0, m]

        w_last[...] = k_in[1]
        coefficients()

    in_copies = [remote(h_out.at[f], r_in.at[slot_in, f], r_send.at[f], r_recv.at[slot_in, f], gz=inward) for f in range(4)]
    out_copies = [remote(fr.at[f, first], r_in.at[1, f], x_send.at[f], r_recv.at[1, f], gz=outward) for f in range(4)]
    stores = [pltpu.make_async_copy(fr.at[f], out.at[f], out_sem.at[f]) for f in range(4)]

    def wait_in(slot, f):
        remote(h_out.at[f], r_in.at[slot, f], r_send.at[f], r_recv.at[slot, f], gz=other_z).wait_recv()

    @pl.when(has_out)
    def _():
        for f in range(2):
            wait_in(0, f)
            fr[f, first] = fr[f, first] + k_in[0] * r_in[0, f]

    def forward(t, g):
        k = first + step * t
        ratio = rat[0, k]
        new = tuple(fr[f, k] + ratio * g[f] for f in range(2))
        for f in range(2):
            fr[f, k] = new[f]
        return new

    g = lax.fori_loop(1, levels, forward, (fr[0, first], fr[1, first]))
    for f in range(2):
        h_out[f] = k_out[0] * g[f]
        in_copies[f].start()

    s_acc[...] = jnp.zeros_like(s_acc)
    h_acc[...] = jnp.zeros_like(h_acc)
    for p in range(gz_n - 1):

        @pl.when(z > p)
        def _(p=p):
            s_copy(1, p).wait_recv()
            s_acc[...] = s_acc[...] + s_in[p]
            h_copy(1, p).wait_recv()
            h_acc[...] = h_acc[...] + h_in[p]

    edge_p[0] = to_column(h_acc[2 * blocks + 1:2 * blocks + 2, :]) + running(dens_n) - 0.5 * dens_n
    p_s = to_column(h_acc[2 * blocks:2 * blocks + 1, :]) + running(dens_s) - 0.5 * dens_s
    p_o = s_acc[:, 0:1] + running(dens_o) - 0.5 * dens_o
    edge_p[1] = as_float(wet_s) * (p_o - p_s)

    sign = jnp.where(down, 1.0, -1.0).astype(F32)
    own = jnp.where(down, 0.0, 1.0).astype(F32)

    def wide_row(ref, r):
        return jnp.concatenate([ref[r * blocks + b:r * blocks + b + 1, :] for b in range(blocks)], axis=1)

    run_ref[...] = s_acc[...] + own * s_src[...]
    g_ref[...] = jnp.zeros_like(g_ref)
    run_w = wide_row(h_acc, 0) + own * wide_row(h_src, 0)
    run_e = wide_row(h_acc, 1) + own * wide_row(h_src, 1)
    row_lane = lax.broadcasted_iota(jnp.int32, (8, rows), 1)
    coriolis = 0.3 * (0.5 + ((start_y + row_lane).astype(F32) + 0.5) / total_y)
    load_wind.wait()
    for copy in v_copies:
        copy.wait_recv()

    def advance(t, carry):
        run_w, run_e = carry
        k = first + step * t
        kg = base + k
        at = pl.ds(k, 1)
        to_north, to_south = 127 - k, lax.rem(128 - k, 128)
        ch, ct = where_rows(t)
        w = [hx[0, ch, f, ct, :] for f in range(3)] + [hv[0, at, :]]
        e = [hx[1, ch, f, ct, :] for f in range(3)] + [hv[1, at, :]]
        aw, bw = take_w[0, at, :], take_w[1, at, :]
        dens_w = density_of(w[0], w[1]) * as_float(kg < dep_w)
        dens_e = density_of(e[0], e[1]) * as_float(kg < dep_e)
        p_w = run_w + (0.5 * sign) * dens_w
        p_e = run_e + (0.5 * sign) * dens_e
        top = jnp.where(kg == 0, 1.0, 0.0).astype(F32)

        def pressure(i):
            sp = spans[i]
            dens = density_of(st[0, k, sp, :], st[1, k, sp, :]) * as_float(kg < depths[0, sp])
            run = run_ref[sp, :]
            run_ref[sp, :] = run + sign * dens
            return run + (0.5 * sign) * dens

        east_p = Easts(pressure, p_e)
        west_p = Wests(as_float(kg < least_w) * (east_p.ahead[0:1] - p_w))
        east_of = [Easts(lambda i, f=f: st[f, k, spans[i], :], e[f]) for f in (2, 3)]
        west_of = [Wests(aw * w[f] + bw * st[f, k, 0:1, :]) for f in (2, 3)]
        for i in range(tiles):
            sp = spans[i]
            coefs = [take[n, k, sp, :] for n in range(4)]
            wet = as_float(kg < depths[0, sp])
            p, p_east = east_p.next(i)
            g_x = as_float(kg < depths[1, sp]) * (p_east - p)
            g_y = as_float(kg < depths[2, sp]) * (tile_north(p, pltpu.roll(edge_p[0, sp], to_north, 1)) - p)
            g_x = g_x + west_p.next(g_x)
            g_y = g_y + tile_south(g_y, pltpu.roll(edge_p[1, sp], to_south, 1))
            (u, u_e), (v, v_e) = east_of[0].next(i), east_of[1].next(i)
            ratio = rat[1, k, sp, :]
            new_u = moved_of(2, i, u, u_e, west_of[0], to_north, to_south, *coefs)
            new_u = (new_u + coriolis * v - 0.015 * g_x + top * wind_ref[0, sp, :]) * wet + ratio * g_ref[0, sp, :]
            g_ref[0, sp, :] = new_u
            fr[2, k, sp, :] = new_u
            new_v = moved_of(3, i, v, v_e, west_of[1], to_north, to_south, *coefs)
            new_v = (new_v - coriolis * u - 0.015 * g_y + top * wind_ref[1, sp, :]) * wet + ratio * g_ref[1, sp, :]
            g_ref[1, sp, :] = new_v
            fr[3, k, sp, :] = new_v
        return run_w + sign * dens_w, run_e + sign * dens_e

    lax.fori_loop(0, levels, advance, (run_w, run_e))

    @pl.when(mid)
    def _():
        remote(c_out, c_in.at[1], c_send, c_recv.at[1], gz=other_z).wait_recv()

    receives_mixing = z > half

    @pl.when(receives_mixing)
    def _():
        mixing_copy(other_z).wait_recv()

    for m in range(2):

        @pl.when(down & jnp.logical_not(mid))
        def _(m=m):
            c = below(m)
            over = 1.0 / (d_last[m] + c)
            k_a[m] = over
            k_b[m] = c * over

        @pl.when(receives_mixing)
        def _(m=m):
            c = mh[m] * as_float(base < dep)
            over = 1.0 / (d_last[m] + c)
            k_a[m] = over
            k_b[m] = c * over

        @pl.when(z == half - 1)
        def _(m=m):
            c = below(m)
            ratio = c / (c_in[1, m] + c)
            over = 1.0 / (d_last[m] + ratio * c_in[1, m])
            k_a[m] = over
            k_b[m] = ratio * over

        @pl.when(z == half)
        def _(m=m):
            over = 1.0 / (d_last[m] + c_in[1, m])
            k_a[m] = over
            k_b[m] = over

    def backward_tracers():
        for f in range(2):
            wait_in(1, f)
            fr[f, final] = k_a[0] * fr[f, final] + k_b[0] * r_in[1, f]

        def backward(t, x):
            k = final - step * t
            ratio, over = rat[0, k + step], inv[0, k]
            new = tuple(over * fr[f, k] + ratio * x[f] for f in range(2))
            for f in range(2):
                fr[f, k] = new[f]
            return new

        lax.fori_loop(1, levels, backward, (fr[0, final], fr[1, final]))
        for f in range(2):

            @pl.when(has_out)
            def _(f=f):
                out_copies[f].start()

            stores[f].start()

    @pl.when(has_out)
    def _():
        backward_tracers()

    for f in (2, 3):

        @pl.when(has_out)
        def _(f=f):
            wait_in(0, f)
            fr[f, final] = fr[f, final] + w_last[...] * r_in[0, f]

        h_out[f] = k_out[1] * fr[f, final]
        in_copies[f].start()

    @pl.when(jnp.logical_not(has_out))
    def _():
        backward_tracers()

    for f in (2, 3):
        wait_in(1, f)
        came = r_in[0, f]
        x = k_a[1] * fr[f, final] + k_b[1] * r_in[1, f]
        fr[f, final] = x

        def backward(t, x, f=f, came=came):
            k = final - step * t
            x = inv[1, k] * fr[f, k] + rat[1, k + step] * x + via[k] * came
            fr[f, k] = x
            return x

        lax.fori_loop(1, levels, backward, x)

        @pl.when(has_out)
        def _(f=f):
            out_copies[f].start()

        stores[f].start()

    for copy in x_copies[0] + x_copies[1] + v_copies:
        copy.wait_send()
    for side, present in ((0, has_north), (1, has_south)):

        @pl.when(present)
        def _(side=side):
            y_copies[side].wait_send()

    for d in range(1, gz_n):

        @pl.when(z + d < gz_n)
        def _(d=d):
            s_copy(d, z).wait_send()
            h_copy(d, z).wait_send()

    @pl.when(sends_mixing)
    def _():
        mixing_copy(z + 1).wait_send()

    c_copy.wait_send()
    for f in range(4):
        in_copies[f].wait_send()

        @pl.when(has_out)
        def _(f=f):
            out_copies[f].wait_send()

        stores[f].wait()


def place(source, target, held, in_sem, out_sem):
    part = source.shape[1] // 2
    pieces = [(f, h) for f in range(4) for h in range(2)]
    ins = [
        pltpu.make_async_copy(source.at[f, pl.ds(h * part, part)], held.at[f, pl.ds(h * part, part)], in_sem.at[f, h])
        for f, h in pieces
    ]
    outs = [
        pltpu.make_async_copy(held.at[f, pl.ds(h * part, part)], target.at[f, pl.ds(h * part, part)], out_sem.at[f, h])
        for f, h in pieces
    ]
    for copy in ins:
        copy.start()
    for arrived, leaving in zip(ins, outs):
        arrived.wait()
        leaving.start()
    for copy in outs:
        copy.wait()


def per_device(sizes, state, mixing, depth_levels, wind):
    _, levels, cols, rows = state.shape
    gz_n = sizes[2]
    blocks = rows // 128
    any_spec = pl.BlockSpec(memory_space=pl.ANY)
    vmem = lambda *shape: pltpu.VMEM(shape, F32)
    dma = lambda *shape: pltpu.SemaphoreType.DMA(shape)
    tile = (cols, rows)
    earlier = max(gz_n - 1, 1)
    h_rows = 8 * pl.cdiv(2 * blocks + 3, 8)
    one = pltpu.SemaphoreType.DMA
    scratch = [
        pltpu.VMEM(depth_levels.shape, jnp.int32), vmem(2, *tile),
        vmem(4, levels, *tile), vmem(2, levels, *tile), vmem(4, levels, *tile),
        vmem(2, levels, *tile), vmem(2, levels, *tile),
        vmem(4, levels, *tile), vmem(2, levels, rows), vmem(levels, *tile), vmem(*tile),
        pltpu.VMEM((3, *tile), jnp.int32), vmem(*tile), vmem(2, *tile),
        vmem(2, 2, 3, levels // 2, rows), vmem(2, 2, 3, levels // 2, rows), vmem(2, levels, rows), vmem(2, levels, rows),
        vmem(2, 4, cols, 128), vmem(2, 4, cols, 128),
        vmem(4, cols, 128), vmem(2, cols, 128),
        vmem(*tile), vmem(earlier, *tile), vmem(*tile),
        vmem(h_rows, 128), vmem(earlier, h_rows, 128), vmem(h_rows, 128),
        vmem(2, *tile), vmem(2, 2, *tile), vmem(2, *tile), vmem(4, *tile), vmem(2, 4, *tile),
        vmem(2, *tile), vmem(2, *tile), vmem(2, *tile), vmem(2, *tile), vmem(2, *tile),
        one, one, dma(4), one, dma(4), dma(2, 2), dma(2, 2), dma(2), dma(2), dma(2), dma(2),
        dma(earlier), dma(earlier), dma(earlier), dma(earlier), one, dma(2), one, one, dma(4), dma(2, 4), dma(4),
    ]
    solved = pl.pallas_call(
        functools.partial(kernel, sizes),
        out_shape=jax.ShapeDtypeStruct(state.shape, F32),
        in_specs=[any_spec] * 4,
        out_specs=any_spec,
        scratch_shapes=scratch,
        compiler_params=pltpu.CompilerParams(
            collective_id=0, has_side_effects=True, vmem_limit_bytes=60 * 1024 * 1024
        ),
        cost_estimate=pl.CostEstimate(flops=state.size * 60, bytes_accessed=state.size * 10, transcendentals=0),
    )(state, mixing, depth_levels, wind)
    return pl.pallas_call(
        place,
        out_shape=jax.ShapeDtypeStruct(state.shape, F32),
        in_specs=[any_spec],
        out_specs=any_spec,
        scratch_shapes=[vmem(*state.shape), dma(4, 2), dma(4, 2)],
        compiler_params=pltpu.CompilerParams(vmem_limit_bytes=60 * 1024 * 1024),
        cost_estimate=pl.CostEstimate(flops=0, bytes_accessed=state.size * 8, transcendentals=0),
    )(solved)


def solution(mesh):
    sizes = tuple(mesh.shape[name] for name in ("gx", "gy", "gz"))
    return jax.shard_map(
        functools.partial(per_device, sizes),
        mesh=mesh,
        in_specs=(P(None, "gz", "gx", "gy"), P(None, "gz", "gx", "gy"), P(), P(None, "gx", "gy")),
        out_specs=P(None, "gz", "gx", "gy"),
        check_vma=False,
    )
```
